128 devices in a mesh: member: 8 (over y_lo, z), space: 16 (over y_hi, x, core).
Axes of the slice: x: 4, y: 4 (y_hi: 2, y_lo: 2; y = y_hi * 2 + y_lo), z: 4, core: 2. Of those that a mesh axis runs over, the one named last changes fastest.
Arguments:
- latent_state: bfloat16 [64, 128, 640], P('space'), may hold values from -6 to 6
- member_noise: bfloat16 [16, 64, 128, 640], P('member', 'space'), may hold values from -6 to 6
- conv_weight: float32 [9, 640], replicated, may hold values from -2 to 2
- norm_gain: float32 [640], replicated, may hold values from 0.1 to 1.9
- weight_in: bfloat16 [1920, 640], replicated, may hold values from -0.25 to 0.25
- weight_down: bfloat16 [1920, 640], replicated, may hold values from -0.125 to 0.125
- weight_head: bfloat16 [640, 320], replicated, may hold values from -0.25 to 0.25
- target_field: float32 [64, 128, 320], P('space'), may hold values from -6 to 6
Outputs:
- grad_in: float32 [1920, 640], P(('member', 'space'))
- grad_down: float32 [1920, 640], P(('member', 'space'))
- grad_head: float32 [640, 320], replicated
- grad_gain: float32 [640], replicated
- grad_conv: float32 [9, 640], replicated
The draws below stay inside these ranges and needn't reach their ends.
All inputs are finite; a program needn't handle non-finite values.
Results may differ from the reference program's by a relative error of at most 0.007.
Values may be sent and summed in bfloat16 or wider, within the bound.
A program may use at most 128 MiB of HBM per device.

```python
import math
import jax
import jax.numpy as jnp
from jax import lax

D = 640
FF = 1920
OUTC = 320
LON = 128
MEMBERS = 16
LAT = 64
POINTS = 8192


def level_of(rng, dims, shards, low, high):
    def one(axis_at, blocks):
        heights = jax.random.uniform(jax.random.fold_in(jax.random.fold_in(rng, 6), axis_at), (blocks,), jnp.float32, low / len(shards), high / len(shards))
        return jnp.repeat(jnp.exp(heights), dims[axis_at] // blocks).reshape((-1,) + (1,) * (len(dims) - axis_at - 1))

    level = one(*shards[0])
    for cut in shards[1:]:
        level = level * one(*cut)
    return level


def bell_draw(stream_key, dims, width, limit, cuts=(), kind=jnp.bfloat16):
    values = jax.random.normal(stream_key, dims, jnp.float32) * width
    if len(cuts) > 0:
        values = level_of(stream_key, dims, cuts, -0.22, 0.18) * values
    return jnp.clip(values, min=-limit, max=limit).astype(kind)


def setup_inputs(seed: int = 0) -> dict:
    keys = jax.random.split(jax.random.key(seed), 9)
    latent_state = bell_draw(keys[0], (LAT, LON, D), 1.0, 6.0, ((0, 16),))
    member_noise = bell_draw(keys[1], (MEMBERS, LAT, LON, D), 1.0, 6.0, ((0, 8), (1, 16)))
    conv_weight = bell_draw(keys[2], (9, D), 9 ** -0.5, 2.0, (), jnp.float32)
    norm_gain = jnp.clip(1.0 + 0.18 * jax.random.normal(keys[3], (D,), jnp.float32), 0.1, 1.9)
    weight_in = bell_draw(keys[4], (FF, D), D ** -0.5, 0.25)
    weight_down = bell_draw(keys[5], (FF, D), FF ** -0.5, 0.125)
    weight_head = bell_draw(keys[6], (D, OUTC), D ** -0.5, 0.25)
    target_field = bell_draw(keys[7], (LAT, LON, OUTC), 1.0, 6.0, ((0, 16),), jnp.float32)
    return dict(latent_state=latent_state, member_noise=member_noise, conv_weight=conv_weight, norm_gain=norm_gain, weight_in=weight_in, weight_down=weight_down, weight_head=weight_head, target_field=target_field)


def pair_pull(own_pred, every_pred):
    gram = jnp.einsum('apc,bpc->abp', own_pred, every_pred, precision=lax.Precision.HIGHEST)
    own_sq = lax.optimization_barrier(jnp.sum(own_pred * own_pred, axis=-1))
    every_sq = lax.optimization_barrier(jnp.sum(every_pred * every_pred, axis=-1))
    inverse = 1.0 / jnp.sqrt(own_sq[:, None, :] + every_sq[None, :, :] - 2.0 * gram + 1.0)
    weight_sum = lax.optimization_barrier(jnp.sum(inverse, axis=1))
    pulled = jnp.einsum('abp,bpc->apc', inverse, every_pred, precision=lax.Precision.HIGHEST)
    return own_pred * weight_sum[..., None] - pulled

def reference(latent_state, member_noise, conv_weight, norm_gain, weight_in, weight_down, weight_head, target_field):
    mixed = (latent_state[None].astype(jnp.float32) + member_noise.astype(jnp.float32)).astype(jnp.bfloat16)
    padded = jnp.pad(mixed, ((0, 0), (1, 1), (0, 0), (0, 0)))
    shifted = [jnp.roll(padded[:, offa:offa + LAT], 1 - offb, axis=2) for offa in range(3) for offb in range(3)]
    conv_out = jnp.zeros(mixed.shape, jnp.float32)
    for index in range(9):
        conv_out = conv_out + conv_weight[index] * shifted[index].astype(jnp.float32)
    total_rows = MEMBERS * POINTS
    conv_rows = conv_out.reshape(total_rows, D)
    center = conv_rows - lax.optimization_barrier(jnp.mean(conv_rows, axis=-1, keepdims=True))
    inv_std = lax.rsqrt(lax.optimization_barrier(jnp.mean(center * center, axis=-1, keepdims=True)) + 1e-05)
    normal = center * inv_std
    normed_b = (normal * norm_gain).astype(jnp.bfloat16)
    contract_last = (((1,), (1,)), ((), ()))
    contract_first = (((0,), (0,)), ((), ()))
    pre_act = lax.dot_general(normed_b, weight_in, contract_last, preferred_element_type=jnp.float32)
    activ_b = jax.nn.gelu(pre_act).astype(jnp.bfloat16)
    hidden_b = (mixed.reshape(total_rows, D).astype(jnp.float32) + jnp.dot(activ_b, weight_down, preferred_element_type=jnp.float32)).astype(jnp.bfloat16)
    predict = jnp.dot(hidden_b, weight_head, preferred_element_type=jnp.float32).reshape(MEMBERS, POINTS, OUTC)
    loss_scale = math.sqrt(MEMBERS * OUTC / POINTS)
    error = predict - target_field.reshape(1, POINTS, OUTC)
    dist_target = jnp.sqrt(lax.optimization_barrier(jnp.sum(error * error, axis=-1, keepdims=True)) + 1.0)
    attract = error / dist_target / MEMBERS
    repulse = pair_pull(predict, predict)
    grad_pred = loss_scale * (attract - repulse / (MEMBERS * (MEMBERS - 1)))
    grad_b = grad_pred.reshape(total_rows, OUTC).astype(jnp.bfloat16)
    grad_head = lax.dot_general(hidden_b, grad_b, contract_first, preferred_element_type=jnp.float32)
    ghid_b = lax.dot_general(grad_b, weight_head, contract_last, preferred_element_type=jnp.float32).astype(jnp.bfloat16)
    grad_down = lax.dot_general(activ_b, ghid_b, contract_first, preferred_element_type=jnp.float32)
    grad_act = lax.dot_general(ghid_b, weight_down, contract_last, preferred_element_type=jnp.float32)
    grad_pre = jax.vjp(jax.nn.gelu, pre_act)[1](grad_act)[0]
    gpre_b = grad_pre.astype(jnp.bfloat16)
    grad_in = lax.dot_general(gpre_b, normed_b, contract_first, preferred_element_type=jnp.float32)
    grad_normed = jnp.dot(gpre_b, weight_in, preferred_element_type=jnp.float32)
    grad_gain = lax.optimization_barrier(jnp.sum(grad_normed * normal, axis=0))
    scaled = grad_normed * norm_gain
    grad_conv_out = (scaled - lax.optimization_barrier(jnp.mean(scaled, axis=-1, keepdims=True)) - normal * lax.optimization_barrier(jnp.mean(scaled * normal, axis=-1, keepdims=True))) * inv_std
    grad_conv4 = grad_conv_out.reshape(mixed.shape)
    grad_conv = jnp.stack([lax.optimization_barrier(jnp.sum(shifted[index].astype(jnp.float32) * grad_conv4, axis=(0, 1, 2))) for index in range(9)])
    return (grad_in, grad_down, grad_head, grad_gain, grad_conv)
```

```python
import functools
import math

import jax
import jax.numpy as jnp
from jax import lax
from jax.experimental import pallas as pl
from jax.experimental.pallas import tpu as pltpu
from jax.sharding import PartitionSpec as P

BF = jnp.bfloat16
F32 = jnp.float32
MESH = pl.DeviceIdType.MESH

MEM = 2
LATD = 4
LON = 128
D = 640
OUTC = 320
FFR = 1920
FF = 2048
ROWS = MEM * LON
MEMBERS = 16
POINTS = 8192
SCALE = math.sqrt(MEMBERS * OUTC / POINTS)
GC = math.sqrt(2.0 / math.pi)
GROUP = [(dz, dy) for dz in range(4) for dy in range(2)][1:]
CHUNKS = [
    ("down", 512, 128, "zxy"),
    ("down", 0, 256, "xyz"),
    ("down", 256, 256, "yzx"),
    ("in", 0, 256, "xyz"),
    ("in", 256, 256, "yzx"),
    ("in", 512, 128, "zxy"),
]
WIDTH = [256, 256, 256, 256, 256, 128]
HEAD_TILES = 120


def dot(a, b, ca, cb):
    return lax.dot_general(a, b, (((ca,), (cb,)), ((), ())), preferred_element_type=F32)


def scratch():
    out = {
        "noise": pltpu.VMEM((LATD, MEM, LON, D), BF),
        "latent": pltpu.VMEM((LATD, LON, D), BF),
        "wraw": pltpu.VMEM((FFR, D), BF),
        "win": pltpu.VMEM((FF, D), BF),
        "wdn": pltpu.VMEM((FF, D), BF),
        "whd": pltpu.VMEM((D, OUTC), BF),
        "tgt": pltpu.VMEM((LATD, 16, OUTC), F32),
        "mixed": pltpu.VMEM((LATD + 2, MEM, LON, D), BF),
        "cbuf": pltpu.VMEM((ROWS, D), F32),
        "normal": pltpu.VMEM((LATD, ROWS, D), F32),
        "istd": pltpu.VMEM((LATD, ROWS, 128), F32),
        "normed": pltpu.VMEM((LATD * ROWS, D), BF),
        "slope": pltpu.VMEM((LATD * ROWS, FF), F32),
        "activ": pltpu.VMEM((LATD * ROWS, FF), BF),
        "gpre": pltpu.VMEM((LATD * ROWS, FF), BF),
        "hidden": pltpu.VMEM((LATD * ROWS, D), BF),
        "ghid": pltpu.VMEM((LATD * ROWS, D), BF),
        "ysend": pltpu.VMEM((LATD, MEM, LON, OUTC), BF),
        "yrecv": pltpu.VMEM((LATD, MEMBERS, 16, OUTC), BF),
        "gsend": pltpu.VMEM((LATD, MEMBERS, 16, OUTC), BF),
        "grecv": pltpu.VMEM((LATD, MEM, LON, OUTC), BF),
        "cacc": pltpu.VMEM((10, 8, D), F32),
        "hall": pltpu.VMEM((2, 4, 4, 4, 16, 128), F32),
        "arc": pltpu.VMEM((2, 10, D), F32),
        "arx": pltpu.VMEM((4, 10, D), F32),
        "ary": pltpu.VMEM((4, 10, D), F32),
        "arz": pltpu.VMEM((4, 10, D), F32),
        "l_sem": pltpu.SemaphoreType.DMA((LATD + 5,)),
        "h_ss": pltpu.SemaphoreType.DMA((2,)),
        "h_rs": pltpu.SemaphoreType.DMA((2,)),
        "y_ss": pltpu.SemaphoreType.DMA((LATD, 7)),
        "y_rs": pltpu.SemaphoreType.DMA((LATD, 7)),
        "g_ss": pltpu.SemaphoreType.DMA((LATD, 7)),
        "g_rs": pltpu.SemaphoreType.DMA((LATD, 7)),
        "r_ss": pltpu.SemaphoreType.DMA((6, 10)),
        "r_rs": pltpu.SemaphoreType.DMA((6, 10)),
        "ag_ss": pltpu.SemaphoreType.DMA((10,)),
        "ag_rs": pltpu.SemaphoreType.DMA((10,)),
        "ar_ss": pltpu.SemaphoreType.DMA((10,)),
        "ar_rs": pltpu.SemaphoreType.DMA((10,)),
    }
    for k, w in enumerate(WIDTH):
        out[f"T{k}"] = pltpu.VMEM((2, 4, 4, 4, 16, w), BF)
        out[f"Ra{k}"] = pltpu.VMEM((4, 4, 4, 16, w), BF)
        out[f"Sb{k}"] = pltpu.VMEM((3, 4, 4, 16, w), BF)
        out[f"Rb{k}"] = pltpu.VMEM((3, 4, 4, 16, w), BF)
        out[f"Sc{k}"] = pltpu.VMEM((4, 4, 16, w), F32)
        out[f"Rc{k}"] = pltpu.VMEM((3, 4, 16, w), F32)
        out[f"Sd{k}"] = pltpu.VMEM((4, 16, w), F32)
        out[f"Rd{k}"] = pltpu.VMEM((3, 16, w), F32)
    return out


NAMES = list(scratch())


def kernel(
    lat_hbm, noise_hbm, cw_ref, gain_ref, win_hbm, wdn_hbm, whd_hbm, tgt_hbm,
    gin_out, gdn_out, head_out, gain_out, conv_out, *refs,
):
    s = dict(zip(NAMES, refs))
    member = lax.axis_index("member")
    space = lax.axis_index("space")
    ylo, z = member // 4, member % 4
    yhi, x, core = space // 8, (space // 2) % 4, space % 2
    y = yhi * 2 + ylo
    at = {"x": x, "y": y, "z": z, "c": core}

    def place(x_, y_, z_, c_):
        return ((y_ % 2) * 4 + z_, (y_ // 2) * 8 + x_ * 2 + c_)

    def partner(axis, step):
        c = dict(at)
        size = 2 if axis == "c" else 4
        c[axis] = (c[axis] + step) % size
        return place(c["x"], c["y"], c["z"], c["c"])

    def mate(dz, dy):
        return ((ylo + dy) % 2) * 4 + (z + dz) % 4

    def halo(step):
        return (member, (space + step) % 16)

    def remote(src, dst, ss, rs, dev):
        return pltpu.make_async_remote_copy(
            src_ref=src, dst_ref=dst, send_sem=ss, recv_sem=rs, device_id=dev, device_id_type=MESH
        )

    barrier = pltpu.get_barrier_semaphore()
    friends = [(mate(dz, dy), space) for dz, dy in GROUP]
    friends += [partner("c", 1), halo(1), halo(-1)]
    friends += [partner(a, j) for a in "xy" for j in (1, 2, 3)]
    for dev in friends:
        pl.semaphore_signal(barrier, inc=1, device_id=dev, device_id_type=MESH)

    lsem = s["l_sem"]
    lat_cp = pltpu.make_async_copy(lat_hbm, s["latent"], lsem.at[LATD])
    noise_cp = [
        pltpu.make_async_copy(noise_hbm.at[:, i], s["noise"].at[i], lsem.at[i]) for i in range(LATD)
    ]
    win_cp = pltpu.make_async_copy(win_hbm, s["wraw"], lsem.at[LATD + 1])
    wdn_cp = pltpu.make_async_copy(wdn_hbm, s["wraw"], lsem.at[LATD + 2])
    whd_cp = pltpu.make_async_copy(whd_hbm, s["whd"], lsem.at[LATD + 3])
    mine16 = pl.ds(pl.multiple_of(member * 16, 16), 16)
    tgt_cp = pltpu.make_async_copy(tgt_hbm.at[:, mine16], s["tgt"], lsem.at[LATD + 4])
    lat_cp.start()
    for i in (0, 3, 1, 2):
        noise_cp[i].start()
    win_cp.start()
    whd_cp.start()
    tgt_cp.start()

    mixed = s["mixed"]

    def mix(i):
        noise_cp[i].wait()
        base = s["latent"][i].astype(F32)
        for m in range(MEM):
            mixed[i + 1, m] = (base + s["noise"][i, m].astype(F32)).astype(BF)

    halo_cp = [
        remote(mixed.at[1], mixed.at[5], s["h_ss"].at[0], s["h_rs"].at[0], halo(-1)),
        remote(mixed.at[4], mixed.at[0], s["h_ss"].at[1], s["h_rs"].at[1], halo(1)),
    ]
    lat_cp.wait()
    mix(0)
    mix(3)
    pl.semaphore_wait(barrier, len(friends))
    for cp in halo_cp:
        cp.start()
    mix(1)
    mix(2)

    row_at = lax.broadcasted_iota(jnp.int32, (256, 240), 0)
    col_at = lax.broadcasted_iota(jnp.int32, (256, 240), 1)
    spread = jnp.where(
        (row_at % 16 < 15) & (col_at == (row_at // 16) * 15 + row_at % 16), 1.0, 0.0
    ).astype(BF)

    def pad_rows(dst):
        for b in range(8):
            dst[256 * b : 256 * b + 256, :] = dot(
                spread, s["wraw"][240 * b : 240 * b + 240, :], 1, 0
            ).astype(BF)

    win_cp.wait()
    pad_rows(s["win"])
    wdn_cp.start()
    s["cacc"][...] = jnp.zeros((10, 8, D), F32)
    wdn_cp.wait()
    pad_rows(s["wdn"])
    whd_cp.wait()
    tgt_cp.wait()

    def y_copy(ci, k):
        dz, dy = GROUP[k]
        to = mate(dz, dy)
        return remote(
            s["ysend"].at[ci, :, pl.ds(pl.multiple_of(to * 16, 16), 16)],
            s["yrecv"].at[ci, pl.ds(member * 2, 2)],
            s["y_ss"].at[ci, k], s["y_rs"].at[ci, k], (to, space),
        )

    def g_copy(ci, k):
        dz, dy = GROUP[k]
        to = mate(dz, dy)
        return remote(
            s["gsend"].at[ci, pl.ds(to * 2, 2)],
            s["grecv"].at[ci, :, mine16],
            s["g_ss"].at[ci, k], s["g_rs"].at[ci, k], (to, space),
        )

    gain = gain_ref[...]

    def forward(ci):
        i = (ci + 1) % LATD
        r0 = pl.multiple_of(ci * ROWS, ROWS)
        rows = pl.ds(r0, ROWS)
        for m in range(MEM):
            for lt in range(D // 128):
                lanes = slice(lt * 128, lt * 128 + 128)
                part = [None] * 3
                for a in range(3):
                    cells = mixed[i + a, m, :, lanes].astype(F32)
                    for b in range(3):
                        term = cw_ref[3 * a + b : 3 * a + b + 1, lanes] * cells
                        part[b] = term if a == 0 else part[b] + term
                s["cbuf"][m * LON : (m + 1) * LON, lanes] = (
                    part[1] + pltpu.roll(part[0], 1, 0) + pltpu.roll(part[2], LON - 1, 0)
                )
        for q in range(ROWS // 32):
            here = slice(q * 32, q * 32 + 32)
            conv = s["cbuf"][here, :]
            center = conv - jnp.mean(conv, axis=-1, keepdims=True)
            inv = lax.rsqrt(jnp.mean(center * center, axis=-1, keepdims=True) + 1e-05)
            normal = center * inv
            s["normal"][ci, here, :] = normal
            s["istd"][ci, here, :] = jnp.broadcast_to(inv, (32, 128))
            s["normed"][pl.ds(pl.multiple_of(r0 + q * 32, 32), 32), :] = (normal * gain).astype(BF)
        normed = s["normed"][rows, :]
        for f in range(4):
            cols = slice(f * 512, f * 512 + 512)
            pre = dot(normed, s["win"][cols, :], 1, 1)
            sq = pre * pre
            t = jnp.tanh(pre * (GC + (GC * 0.044715) * sq))
            half = 0.5 + 0.5 * t
            act = pre * half
            s["activ"][rows, cols] = act.astype(BF)
            s["slope"][rows, cols] = half + act * (1.0 - t) * (GC + (3 * GC * 0.044715) * sq)
        down = dot(s["activ"][rows, :], s["wdn"][...], 1, 0)
        base = mixed[i + 1].reshape(ROWS, D).astype(F32)
        hidden = (base + down).astype(BF)
        s["hidden"][rows, :] = hidden
        pred = dot(hidden, s["whd"][...], 1, 0)
        s["ysend"][ci] = pred.astype(BF).reshape(MEM, LON, OUTC)
        s["yrecv"][ci, pl.ds(member * 2, 2)] = s["ysend"][ci, :, mine16]
        for k in range(7):
            y_copy(ci, k).start()

    def score(ci):
        i = (ci + 1) % LATD
        for k in range(7):
            y_copy(ci, k).wait_recv()
        yb = s["yrecv"][ci].reshape(256, OUTC)
        gram = dot(yb, yb, 1, 1)
        r = lax.broadcasted_iota(jnp.int32, (256, 256), 0)
        c = lax.broadcasted_iota(jnp.int32, (256, 256), 1)
        diag = jnp.where(r == c, gram, 0.0)
        sq_r = jnp.sum(diag, axis=1, keepdims=True)
        sq_c = jnp.sum(diag, axis=0, keepdims=True)
        inv = lax.rsqrt(jnp.maximum(sq_r + sq_c - 2.0 * gram + 1.0, 1.0))
        w = jnp.where(r % 16 == c % 16, inv, 0.0).astype(BF)
        w_sum = jnp.sum(w.astype(F32), axis=1, keepdims=True)
        pulled = dot(w, yb, 1, 0)
        yf = yb.astype(F32)
        err = (yf.reshape(16, 16, OUTC) - s["tgt"][i][None]).reshape(256, OUTC)
        far = lax.rsqrt(jnp.sum(err * err, axis=-1, keepdims=True) + 1.0)
        grad = err * (far * (SCALE / MEMBERS)) - (yf * w_sum - pulled) * (
            SCALE / (MEMBERS * (MEMBERS - 1))
        )
        s["gsend"][ci] = grad.astype(BF).reshape(MEMBERS, 16, OUTC)
        s["grecv"][ci, :, mine16] = s["gsend"][ci, pl.ds(member * 2, 2)]
        for k in range(7):
            g_copy(ci, k).start()

    @pl.loop(0, LATD)
    def _(ci):
        @pl.when(ci == 2)
        def _():
            for cp in halo_cp:
                cp.wait()

            @pl.when(space == 0)
            def _():
                mixed[0] = jnp.zeros((MEM, LON, D), BF)

            @pl.when(space == 15)
            def _():
                mixed[5] = jnp.zeros((MEM, LON, D), BF)

        forward(ci)

        @pl.when(ci > 0)
        def _():
            score(ci - 1)

    def order(k):
        return CHUNKS[k][3]

    def rs_copy(k, stage, j=1):
        o = order(k)
        if stage == 0:
            n, src, dst, dev = 0, s[f"T{k}"].at[1 - core], s[f"Ra{k}"], partner("c", 1)
        else:
            pair = {1: ("Sb", "Rb"), 2: ("Sc", "Rc"), 3: ("Sd", "Rd")}[stage]
            n = 3 * (stage - 1) + j
            src, dst = s[f"{pair[0]}{k}"].at[j - 1], s[f"{pair[1]}{k}"].at[j - 1]
            dev = partner(o[stage - 1], j)
        return remote(src, dst, s["r_ss"].at[k, n], s["r_rs"].at[k, n], dev)

    def spot(k, o_ylo, o_z, o_yhi, o_x):
        v = {"x": o_x, "y": o_yhi * 2 + o_ylo, "z": o_z}
        return tuple(v[a] for a in order(k))

    def product(k, left, right):
        _, c0, w, _ = CHUNKS[k]
        T = s[f"T{k}"]

        @pl.loop(0, 2)
        def _(o_ylo):
            half = dot(
                left[:, pl.ds(pl.multiple_of(o_ylo * 1024, 1024), 1024)], right[:, c0 : c0 + w], 0, 0
            ).astype(BF)
            for g in range(64):
                o_z, o_yhi, o_x, o_c = g // 16, (g // 8) % 2, (g // 2) % 4, g % 2
                i1, i2, i3 = spot(k, o_ylo, o_z, o_yhi, o_x)
                T[o_c, i1, i2, i3, :, 0:w] = half[g * 16 : g * 16 + 16, :]

    def head_product(k):
        T = s[f"T{k}"]
        grad = dot(s["hidden"][...], s["grecv"][...].reshape(LATD * ROWS, OUTC), 0, 0).astype(BF)
        for t in range(128):
            i1, i2, i3 = spot(k, t // 64, (t // 16) % 4, (t // 8) % 2, (t // 2) % 4)
            at_ = (t % 2, i1, i2, i3)
            if t >= HEAD_TILES:
                T[(*at_, slice(None), slice(128, 256))] = jnp.zeros((16, 128), BF)
                continue
            rt, ct = t // 3, t % 3
            tile = grad[rt * 16 : rt * 16 + 16, ct * 128 : min(OUTC, ct * 128 + 128)]
            if ct == 2:
                T[(*at_, slice(None), slice(192, 256))] = jnp.zeros((16, 64), BF)
            T[(*at_, slice(None), slice(128, 128 + tile.shape[1]))] = tile

    def stage1(k):
        a1 = at[order(k)[0]]
        T, Ra, Sb = s[f"T{k}"], s[f"Ra{k}"], s[f"Sb{k}"]
        rs_copy(k, 0).wait_recv()
        for j in (1, 2, 3):
            n = (a1 + j) % 4
            Sb[j - 1] = (T[core, n].astype(F32) + Ra[n].astype(F32)).astype(BF)
            rs_copy(k, 1, j).start()

    def stage2(k):
        a1, a2 = at[order(k)[0]], at[order(k)[1]]
        T, Ra, Rb, Sc = s[f"T{k}"], s[f"Ra{k}"], s[f"Rb{k}"], s[f"Sc{k}"]
        for j in (1, 2, 3):
            rs_copy(k, 1, j).wait_recv()
        for j in (1, 2, 3, 4):
            n = (a2 + j) % 4
            total = T[core, a1, n].astype(F32) + Ra[a1, n].astype(F32)
            for i in range(3):
                total = total + Rb[i, n].astype(F32)
            Sc[j - 1] = total
            if j < 4:
                rs_copy(k, 2, j).start()

    def stage3(k):
        a3 = at[order(k)[2]]
        Sc, Rc, Sd = s[f"Sc{k}"], s[f"Rc{k}"], s[f"Sd{k}"]
        for j in (1, 2, 3):
            rs_copy(k, 2, j).wait_recv()
        for j in (1, 2, 3, 4):
            n = (a3 + j) % 4
            Sd[j - 1] = Sc[3, n] + Rc[0, n] + Rc[1, n] + Rc[2, n]
            if j < 4:
                rs_copy(k, 3, j).start()

    def finish(k):
        name, c0, w, _ = CHUNKS[k]
        Sd, Rd = s[f"Sd{k}"], s[f"Rd{k}"]
        for j in (1, 2, 3):
            rs_copy(k, 3, j).wait_recv()
        total = Sd[3] + Rd[0] + Rd[1] + Rd[2]
        out = gdn_out if name == "down" else gin_out
        out[:, c0 : c0 + w] = total[0:15, 0:w]
        return total

    hall = s["hall"]
    h1, h2, h3 = (at[a] for a in order(0))

    def ag_copy(n, j=1):
        part = [hall.at[core, h1, h2, h3], hall.at[core, h1, h2], hall.at[core, h1], hall.at[core]][n]
        dev = partner("c", 1) if n == 3 else partner(order(0)[2 - n], j)
        m = 9 if n == 3 else 3 * n + j - 1
        return remote(part, part, s["ag_ss"].at[m], s["ag_rs"].at[m], dev)

    def ag_start(n):
        for j in (1,) if n == 3 else (1, 2, 3):
            ag_copy(n, j).start()

    def ag_wait(n):
        for j in (1,) if n == 3 else (1, 2, 3):
            ag_copy(n, j).wait_recv()

    def ar_copy(n, j=1):
        axis = "cxyz"[n]
        buf = s["ar" + axis]
        m = 0 if n == 0 else 3 * n - 3 + j
        part = buf.at[at[axis]]
        return remote(part, part, s["ar_ss"].at[m], s["ar_rs"].at[m], partner(axis, j))

    def ar_start(n, value):
        axis = "cxyz"[n]
        s["ar" + axis][at[axis]] = value
        for j in (1,) if n == 0 else (1, 2, 3):
            ar_copy(n, j).start()

    def ar_sum(n):
        buf = s["ar" + "cxyz"[n]]
        for j in (1,) if n == 0 else (1, 2, 3):
            ar_copy(n, j).wait_recv()
        total = buf[0]
        for i in range(1, 2 if n == 0 else 4):
            total = total + buf[i]
        return total

    def grad_hidden(ci):
        rows = pl.ds(pl.multiple_of(ci * ROWS, ROWS), ROWS)
        for k in range(7):
            g_copy(ci, k).wait_recv()
        s["ghid"][rows, :] = dot(
            s["grecv"][ci].reshape(ROWS, OUTC), s["whd"][...], 1, 1
        ).astype(BF)

    def backward(ci):
        i = (ci + 1) % LATD
        rows = pl.ds(pl.multiple_of(ci * ROWS, ROWS), ROWS)
        ghid = s["ghid"][rows, :]
        for f in range(4):
            cols = slice(f * 512, f * 512 + 512)
            gact = dot(ghid, s["wdn"][cols, :], 1, 1)
            s["gpre"][rows, cols] = (s["slope"][rows, cols] * gact).astype(BF)
        s["cbuf"][...] = dot(s["gpre"][rows, :], s["win"][...], 1, 0)
        gain_acc = jnp.zeros((8, D), F32)
        for q in range(ROWS // 32):
            here = slice(q * 32, q * 32 + 32)
            gn = s["cbuf"][here, :]
            normal = s["normal"][ci, here, :]
            inv = s["istd"][ci, here, 0:1]
            gain_acc = gain_acc + jnp.sum((gn * normal).reshape(4, 8, D), axis=0)
            g = gn * gain
            s["cbuf"][here, :] = (
                g
                - jnp.mean(g, axis=-1, keepdims=True)
                - normal * jnp.mean(g * normal, axis=-1, keepdims=True)
            ) * inv
        s["cacc"][9] = s["cacc"][9] + gain_acc
        for lt in range(D // 128):
            lanes = slice(lt * 128, lt * 128 + 128)
            acc = [s["cacc"][n, :, lanes] for n in range(9)]
            for m in range(MEM):
                g1 = s["cbuf"][m * LON : (m + 1) * LON, lanes]
                moved = [pltpu.roll(g1, LON - 1, 0), g1, pltpu.roll(g1, 1, 0)]
                for a in range(3):
                    cells = mixed[i + a, m, :, lanes].astype(F32)
                    for b in range(3):
                        acc[3 * a + b] = acc[3 * a + b] + jnp.sum(
                            (cells * moved[b]).reshape(16, 8, 128), axis=0
                        )
            for n in range(9):
                s["cacc"][n, :, lanes] = acc[n]

    @pl.loop(0, LATD)
    def _(ci):
        @pl.when(ci == 1)
        def _():
            score(LATD - 1)

        @pl.when(ci < 2)
        def _():
            grad_hidden(ci)

        @pl.when(ci == 2)
        def _():
            grad_hidden(2)
            grad_hidden(3)
            head_product(0)
            product(0, s["activ"], s["ghid"])
            rs_copy(0, 0).start()
            product(1, s["activ"], s["ghid"])
            rs_copy(1, 0).start()
            stage1(0)
            product(2, s["activ"], s["ghid"])
            rs_copy(2, 0).start()
            stage1(1)

        backward(ci)

        @pl.when(ci == 2)
        def _():
            stage1(2)

    ar_start(0, jnp.sum(s["cacc"][...], axis=1))
    stage2(0)
    product(3, s["gpre"], s["normed"])
    rs_copy(3, 0).start()
    stage2(1)
    ar_start(1, ar_sum(0))
    product(4, s["gpre"], s["normed"])
    rs_copy(4, 0).start()
    stage1(3)
    stage2(2)
    stage3(0)
    product(5, s["gpre"], s["normed"])
    rs_copy(5, 0).start()
    stage1(4)
    ar_start(2, ar_sum(1))
    stage3(1)
    stage1(5)
    stage3(2)
    total = finish(0)
    hall[core, h1, h2, h3] = total[:, 128:256]
    ag_start(0)
    finish(1)
    finish(2)
    ar_start(3, ar_sum(2))
    ag_wait(0)
    ag_start(1)
    stage2(3)
    stage2(4)
    stage2(5)
    ag_wait(1)
    ag_start(2)
    sums = ar_sum(3)
    conv_out[...] = sums[0:9]
    gain_out[...] = sums[9:10]
    stage3(3)
    stage3(4)
    stage3(5)
    ag_wait(2)
    ag_start(3)
    finish(3)
    finish(4)
    finish(5)
    ag_wait(3)
    for t in range(HEAD_TILES):
        i1, i2, i3 = spot(0, t // 64, (t // 16) % 4, (t // 8) % 2, (t // 2) % 4)
        rt, ct = t // 3, t % 3
        n = min(128, OUTC - ct * 128)
        head_out[rt * 16 : rt * 16 + 16, ct * 128 : ct * 128 + n] = hall[t % 2, i1, i2, i3, :, 0:n]

    @pl.loop(0, LATD)
    def _(ci):
        for k in range(7):
            y_copy(ci, k).wait_send()
            g_copy(ci, k).wait_send()

    for k in range(6):
        rs_copy(k, 0).wait_send()
        for stage in (1, 2, 3):
            for j in (1, 2, 3):
                rs_copy(k, stage, j).wait_send()
    for n in range(4):
        for j in (1,) if n == 3 else (1, 2, 3):
            ag_copy(n, j).wait_send()
        for j in (1,) if n == 0 else (1, 2, 3):
            ar_copy(n, j).wait_send()


def body(
    latent_state, member_noise, conv_weight, norm_gain, weight_in, weight_down, weight_head, target_field
):
    vmem = pl.BlockSpec(memory_space=pltpu.VMEM)
    hbm = pl.BlockSpec(memory_space=pl.ANY)
    gin, gdn, head, gain, conv = pl.pallas_call(
        kernel,
        name="ensemble_block",
        out_shape=(
            jax.ShapeDtypeStruct((15, D), F32),
            jax.ShapeDtypeStruct((15, D), F32),
            jax.ShapeDtypeStruct((D, OUTC), F32),
            jax.ShapeDtypeStruct((1, D), F32),
            jax.ShapeDtypeStruct((9, D), F32),
        ),
        in_specs=[hbm, hbm, vmem, vmem, hbm, hbm, hbm, hbm],
        out_specs=(vmem,) * 5,
        scratch_shapes=list(scratch().values()),
        compiler_params=pltpu.CompilerParams(
            collective_id=0, has_side_effects=True, vmem_limit_bytes=62 * 2**20
        ),
        cost_estimate=pl.CostEstimate(
            flops=17_000_000_000, bytes_accessed=9_000_000, transcendentals=2_100_000
        ),
    )(
        latent_state, member_noise, conv_weight, norm_gain.reshape(1, D), weight_in, weight_down,
        weight_head, target_field,
    )
    return gin, gdn, head, gain.reshape(D), conv


def solution(mesh):
    return jax.shard_map(
        body,
        mesh=mesh,
        in_specs=(
            P("space", None, None),
            P("member", "space", None, None),
            P(),
            P(),
            P(),
            P(),
            P(),
            P("space", None, None),
        ),
        out_specs=(P(("member", "space"), None), P(("member", "space"), None), P(), P(), P()),
        check_vma=False,
    )
```

```python
import functools
import math

import jax
import jax.numpy as jnp
from jax import lax
from jax.experimental import pallas as pl
from jax.experimental.pallas import tpu as pltpu
from jax.sharding import PartitionSpec as P

BF = jnp.bfloat16
F32 = jnp.float32
MESH = pl.DeviceIdType.MESH

MEM = 2
LATD = 4
LON = 128
D = 640
OUTC = 320
FFR = 1920
FF = 2048
ROWS = MEM * LON
MEMBERS = 16
POINTS = 8192
SCALE = math.sqrt(MEMBERS * OUTC / POINTS)
GC = math.sqrt(2.0 / math.pi)
GROUP = [(dz, dy) for dz in range(4) for dy in range(2)][1:]
CHUNKS = [
    ("head", 0, 128, "zxy"),
    ("down", 0, 256, "xyz"),
    ("down", 256, 256, "yzx"),
    ("down", 512, 128, "zxy"),
    ("in", 0, 256, "xyz"),
    ("in", 256, 256, "yzx"),
    ("in", 512, 128, "zxy"),
]
HEAD_TILES = 100


def dot(a, b, ca, cb):
    return lax.dot_general(a, b, (((ca,), (cb,)), ((), ())), preferred_element_type=F32)


def scratch():
    out = {
        "win": pltpu.VMEM((FF, D), BF),
        "wdn": pltpu.VMEM((FF, D), BF),
        "whd": pltpu.VMEM((OUTC, D), BF),
        "tgt": pltpu.VMEM((LATD, LON, OUTC), F32),
        "mixed": pltpu.VMEM((LATD + 2, MEM, LON, D), BF),
        "cbuf": pltpu.VMEM((2 * ROWS, D), F32),
        "normal": pltpu.VMEM((LATD + 1, ROWS, D), F32),
        "istd": pltpu.VMEM((LATD + 1, ROWS, 128), F32),
        "normed": pltpu.VMEM(((LATD + 1) * ROWS, D), BF),
        "slope": pltpu.VMEM((LATD * ROWS, FF), F32),
        "activ": pltpu.VMEM((LATD * ROWS, FF), BF),
        "gpre": pltpu.VMEM((LATD * ROWS, FF), BF),
        "hidden": pltpu.VMEM((LATD * ROWS, D), BF),
        "ghid": pltpu.VMEM((LATD * ROWS, D), BF),
        "ysend": pltpu.VMEM((LATD, MEM, LON, OUTC), BF),
        "yrecv": pltpu.VMEM((LATD, MEMBERS, 16, OUTC), BF),
        "gsend": pltpu.VMEM((LATD, MEMBERS, 16, OUTC), BF),
        "grecv": pltpu.VMEM((LATD, MEM, LON, OUTC), BF),
        "cacc": pltpu.VMEM((10, 8, D), F32),
        "hall": pltpu.VMEM((2, 4, 4, 4, 16, 128), BF),
        "arc": pltpu.VMEM((2, 10, D), F32),
        "arx": pltpu.VMEM((4, 10, D), F32),
        "ary": pltpu.VMEM((4, 10, D), F32),
        "arz": pltpu.VMEM((4, 10, D), F32),
        "cw": pltpu.VMEM((9, D), F32),
        "gain": pltpu.VMEM((D,), F32),
        "o_gin": pltpu.VMEM((15, D), F32),
        "o_gdn": pltpu.VMEM((15, D), F32),
        "o_head": pltpu.VMEM((OUTC, D), F32),
        "o_gain": pltpu.VMEM((D,), F32),
        "o_conv": pltpu.VMEM((9, D), F32),
        "o_sem": pltpu.SemaphoreType.DMA((5,)),
        "l_sem": pltpu.SemaphoreType.DMA((LATD + 3,)),
        "i_sem": pltpu.SemaphoreType.DMA((LATD, MEM + 1)),
        "w_sem": pltpu.SemaphoreType.DMA((2, 8)),
        "h_ss": pltpu.SemaphoreType.DMA((2,)),
        "h_rs": pltpu.SemaphoreType.DMA((2,)),
        "y_ss": pltpu.SemaphoreType.DMA((LATD, 7)),
        "y_rs": pltpu.SemaphoreType.DMA((LATD, 7)),
        "g_ss": pltpu.SemaphoreType.DMA((LATD, 7)),
        "g_rs": pltpu.SemaphoreType.DMA((LATD, 7)),
        "r_ss": pltpu.SemaphoreType.DMA((7, 10)),
        "r_rs": pltpu.SemaphoreType.DMA((7, 10)),
        "ag_ss": pltpu.SemaphoreType.DMA((10,)),
        "ag_rs": pltpu.SemaphoreType.DMA((10,)),
        "ar_ss": pltpu.SemaphoreType.DMA((10,)),
        "ar_rs": pltpu.SemaphoreType.DMA((10,)),
    }
    for k, (_, _, w, _) in enumerate(CHUNKS):
        out[f"T{k}"] = pltpu.VMEM((2, 4, 4, 4, 16, w), BF)
        out[f"Ra{k}"] = pltpu.VMEM((4, 4, 4, 16, w), BF)
        out[f"Sb{k}"] = pltpu.VMEM((3, 4, 4, 16, w), BF)
        out[f"Rb{k}"] = pltpu.VMEM((3, 4, 4, 16, w), BF)
        out[f"Sc{k}"] = pltpu.VMEM((3, 4, 16, w), BF)
        out[f"Oc{k}"] = pltpu.VMEM((4, 16, w), F32)
        out[f"Rc{k}"] = pltpu.VMEM((3, 4, 16, w), BF)
        out[f"Sd{k}"] = pltpu.VMEM((4, 16, w), F32)
        out[f"Rd{k}"] = pltpu.VMEM((3, 16, w), F32)
    return out


NAMES = list(scratch())


def kernel(
    lat_hbm, noise_hbm, cw_hbm, gain_hbm, win_hbm, wdn_hbm, whd_hbm, tgt_hbm,
    gin_hbm, gdn_hbm, head_hbm, ggain_hbm, gconv_hbm, *refs,
):
    s = dict(zip(NAMES, refs))
    member = lax.axis_index("member")
    space = lax.axis_index("space")
    ylo, z = member // 4, member % 4
    yhi, x, core = space // 8, (space // 2) % 4, space % 2
    y = yhi * 2 + ylo
    at = {"x": x, "y": y, "z": z, "c": core}

    def place(x_, y_, z_, c_):
        return ((y_ % 2) * 4 + z_, (y_ // 2) * 8 + x_ * 2 + c_)

    def partner(axis, step):
        c = dict(at)
        size = 2 if axis == "c" else 4
        c[axis] = (c[axis] + step) % size
        return place(c["x"], c["y"], c["z"], c["c"])

    def mate(dz, dy):
        return ((ylo + dy) % 2) * 4 + (z + dz) % 4

    def halo(step):
        return (member, (space + step) % 16)

    def remote(src, dst, ss, rs, dev):
        return pltpu.make_async_remote_copy(
            src_ref=src, dst_ref=dst, send_sem=ss, recv_sem=rs, device_id=dev, device_id_type=MESH
        )

    barrier = pltpu.get_barrier_semaphore()
    friends = [(mate(dz, dy), space) for dz, dy in GROUP]
    friends += [partner("c", 1), halo(1), halo(-1)]
    friends += [partner(a, j) for a in "xy" for j in (1, 2, 3)]
    for dev in friends:
        pl.semaphore_signal(barrier, inc=1, device_id=dev, device_id_type=MESH)

    lsem = s["l_sem"]

    def cells_raw(i, m):
        n = (i * MEM + m) * LON
        return s["hidden"].at[n : n + LON]

    def latent_raw(i):
        return s["ghid"].at[i * LON : i * LON + LON]

    cells_cp = [
        [
            pltpu.make_async_copy(noise_hbm.at[m, i], cells_raw(i, m), s["i_sem"].at[i, m])
            for m in range(MEM)
        ]
        + [pltpu.make_async_copy(lat_hbm.at[i], latent_raw(i), s["i_sem"].at[i, MEM])]
        for i in range(LATD)
    ]

    def raw(name, b):
        r, c = (b % 4) * 240, (b // 4) * D
        return s[name].at[r : r + 240, c : c + D]

    win_cp = [
        pltpu.make_async_copy(win_hbm.at[240 * b : 240 * b + 240], raw("activ", b), s["w_sem"].at[0, b])
        for b in range(8)
    ]
    wdn_cp = [
        pltpu.make_async_copy(wdn_hbm.at[240 * b : 240 * b + 240], raw("gpre", b), s["w_sem"].at[1, b])
        for b in range(8)
    ]
    whd_cp = pltpu.make_async_copy(whd_hbm, s["whd"], lsem.at[LATD])

    def traw(i):
        return s["slope"].at[0:OUTC, LON * i : LON * i + LON]

    tgt_cp = [
        pltpu.make_async_copy(tgt_hbm.at[i], traw(i), lsem.at[i]) for i in range(LATD)
    ]
    cw_cp = pltpu.make_async_copy(cw_hbm, s["cw"], lsem.at[LATD + 1])
    gain_cp = pltpu.make_async_copy(gain_hbm, s["gain"], lsem.at[LATD + 2])
    out_cp = [
        pltpu.make_async_copy(s[n], dst, s["o_sem"].at[k])
        for k, (n, dst) in enumerate(
            (
                ("o_gin", gin_hbm),
                ("o_gdn", gdn_hbm),
                ("o_head", head_hbm),
                ("o_gain", ggain_hbm),
                ("o_conv", gconv_hbm),
            )
        )
    ]
    mine16 = pl.ds(pl.multiple_of(member * 16, 16), 16)
    for i in (0, 3, 1, 2):
        for cp in cells_cp[i]:
            cp.start()
    for cp in (cw_cp, gain_cp, *win_cp, *wdn_cp, whd_cp, *tgt_cp):
        cp.start()

    mixed = s["mixed"]

    def mix(i):
        for cp in cells_cp[i]:
            cp.wait()
        base = latent_raw(i)[...].astype(F32)
        for m in range(MEM):
            mixed[i + 1, m] = (base + cells_raw(i, m)[...].astype(F32)).astype(BF)

    halo_cp = [
        remote(mixed.at[1], mixed.at[5], s["h_ss"].at[0], s["h_rs"].at[0], halo(-1)),
        remote(mixed.at[4], mixed.at[0], s["h_ss"].at[1], s["h_rs"].at[1], halo(1)),
    ]
    mix(0)
    mix(3)
    pl.semaphore_wait(barrier, len(friends))
    for cp in halo_cp:
        cp.start()
    mix(1)
    mix(2)

    row_at = lax.broadcasted_iota(jnp.int32, (256, 240), 0)
    col_at = lax.broadcasted_iota(jnp.int32, (256, 240), 1)
    spread = jnp.where(
        (row_at % 16 < 15) & (col_at == (row_at // 16) * 15 + row_at % 16), 1.0, 0.0
    ).astype(BF)

    def pad_rows(dst, name):
        for b in range(8):
            r, c = (b % 4) * 240, (b // 4) * D
            dst[256 * b : 256 * b + 256, :] = dot(
                spread, s[name][r : r + 240, c : c + D], 1, 0
            ).astype(BF)

    def y_copy(ci, k):
        dz, dy = GROUP[k]
        to = mate(dz, dy)
        return remote(
            s["ysend"].at[ci, :, pl.ds(pl.multiple_of(to * 16, 16), 16)],
            s["yrecv"].at[ci, pl.ds(member * 2, 2)],
            s["y_ss"].at[ci, k], s["y_rs"].at[ci, k], (to, space),
        )

    def g_copy(ci, k):
        dz, dy = GROUP[k]
        to = mate(dz, dy)
        return remote(
            s["gsend"].at[ci, pl.ds(to * 2, 2)],
            s["grecv"].at[ci, :, mine16],
            s["g_ss"].at[ci, k], s["g_rs"].at[ci, k], (to, space),
        )


    def conv_norm(ci):
        i = (ci + 1) % LATD
        r0 = pl.multiple_of(ci * ROWS, ROWS)
        for m in range(MEM):
            for lt in range(D // 128):
                lanes = slice(lt * 128, lt * 128 + 128)
                part = [None] * 3
                for a in range(3):
                    cells = mixed[i + a, m, :, lanes].astype(F32)
                    for b in range(3):
                        term = s["cw"][3 * a + b : 3 * a + b + 1, lanes] * cells
                        part[b] = term if a == 0 else part[b] + term
                s["cbuf"][m * LON : (m + 1) * LON, lanes] = (
                    part[1] + pltpu.roll(part[0], 1, 0) + pltpu.roll(part[2], LON - 1, 0)
                )
        for q in range(ROWS // 32):
            here = slice(q * 32, q * 32 + 32)
            conv = s["cbuf"][here, :]
            center = conv - jnp.mean(conv, axis=-1, keepdims=True)
            inv = lax.rsqrt(jnp.mean(center * center, axis=-1, keepdims=True) + 1e-05)
            normal = center * inv
            s["normal"][ci, here, :] = normal
            s["istd"][ci, here, :] = jnp.broadcast_to(inv, (32, 128))
            s["normed"][pl.ds(pl.multiple_of(r0 + q * 32, 32), 32), :] = (normal * gain).astype(BF)

    def mixer(ci):
        i = (ci + 1) % LATD
        rows = pl.ds(pl.multiple_of(ci * ROWS, ROWS), ROWS)
        normed = s["normed"][rows, :]
        for f in range(4):
            cols = slice(f * 512, f * 512 + 512)
            pre = dot(normed, s["win"][cols, :], 1, 1)
            sq = pre * pre
            t = jnp.tanh(pre * (GC + (GC * 0.044715) * sq))
            half = 0.5 + 0.5 * t
            act = pre * half
            s["activ"][rows, cols] = act.astype(BF)
            s["slope"][rows, cols] = half + act * (1.0 - t) * (GC + (3 * GC * 0.044715) * sq)
        down = dot(s["activ"][rows, :], s["wdn"][...], 1, 0)
        base = mixed[i + 1].reshape(ROWS, D).astype(F32)
        hidden = (base + down).astype(BF)
        s["hidden"][rows, :] = hidden
        pred = dot(hidden, s["whd"][...], 1, 1)
        s["ysend"][ci] = pred.astype(BF).reshape(MEM, LON, OUTC)
        s["yrecv"][ci, pl.ds(member * 2, 2)] = s["ysend"][ci, :, mine16]

    def score(ci):
        i = (ci + 1) % LATD
        for k in range(7):
            y_copy(ci, k).wait_recv()
        yb = s["yrecv"][ci].reshape(256, OUTC)
        gram = dot(yb, yb, 1, 1)
        r = lax.broadcasted_iota(jnp.int32, (256, 256), 0)
        c = lax.broadcasted_iota(jnp.int32, (256, 256), 1)
        diag = jnp.where(r == c, gram, 0.0)
        sq_r = jnp.sum(diag, axis=1, keepdims=True)
        sq_c = jnp.sum(diag, axis=0, keepdims=True)
        inv = lax.rsqrt(jnp.maximum(sq_r + sq_c - 2.0 * gram + 1.0, 1.0))
        w = jnp.where(r % 16 == c % 16, inv, 0.0).astype(BF)
        w_sum = jnp.sum(w.astype(F32), axis=1, keepdims=True)
        pulled = dot(w, yb, 1, 0)
        yf = yb.astype(F32)
        err = (yf.reshape(16, 16, OUTC) - s["tgt"][i, mine16, :][None]).reshape(256, OUTC)
        far = lax.rsqrt(jnp.sum(err * err, axis=-1, keepdims=True) + 1.0)
        grad = err * (far * (SCALE / MEMBERS)) - (yf * w_sum - pulled) * (
            SCALE / (MEMBERS * (MEMBERS - 1))
        )
        s["gsend"][ci] = grad.astype(BF).reshape(MEMBERS, 16, OUTC)
        s["grecv"][ci, :, mine16] = s["gsend"][ci, pl.ds(member * 2, 2)]
        for k in range(7):
            g_copy(ci, k).start()

    for cp in (cw_cp, gain_cp):
        cp.wait()
    s["cacc"][...] = jnp.zeros((10, 8, D), F32)
    gain = s["gain"][...].reshape(1, D)
    conv_norm(0)
    for cp in (*win_cp, *wdn_cp, whd_cp, *tgt_cp):
        cp.wait()
    pad_rows(s["win"], "activ")
    pad_rows(s["wdn"], "gpre")
    for i in range(LATD):
        s["tgt"][i] = traw(i)[...].T

    @pl.loop(0, LATD)
    def _(ci):
        @pl.when(ci == 1)
        def _():
            for cp in halo_cp:
                cp.wait()

            @pl.when(space == 0)
            def _():
                mixed[0] = jnp.zeros((MEM, LON, D), BF)

            @pl.when(space == 15)
            def _():
                mixed[5] = jnp.zeros((MEM, LON, D), BF)

        mixer(ci)
        conv_norm(ci + 1)
        for k in range(7):
            y_copy(ci, k).start()

        @pl.when(ci > 0)
        def _():
            score(ci - 1)

    def order(k):
        return CHUNKS[k][3]

    def rs_copy(k, stage, j=1):
        o = order(k)
        if stage == 0:
            n, src, dst, dev = 0, s[f"T{k}"].at[1 - core], s[f"Ra{k}"], partner("c", 1)
        else:
            pair = {1: ("Sb", "Rb"), 2: ("Sc", "Rc"), 3: ("Sd", "Rd")}[stage]
            n = 3 * (stage - 1) + j
            src, dst = s[f"{pair[0]}{k}"].at[j - 1], s[f"{pair[1]}{k}"].at[j - 1]
            dev = partner(o[stage - 1], j)
        return remote(src, dst, s["r_ss"].at[k, n], s["r_rs"].at[k, n], dev)

    def spot(k, o_ylo, o_z, o_yhi, o_x):
        v = {"x": o_x, "y": o_yhi * 2 + o_ylo, "z": o_z}
        return tuple(v[a] for a in order(k))

    def product(k, left, right):
        _, c0, w, _ = CHUNKS[k]
        T = s[f"T{k}"]

        @pl.loop(0, 2)
        def _(o_ylo):
            half = dot(
                left[:, pl.ds(pl.multiple_of(o_ylo * 1024, 1024), 1024)],
                right[0 : LATD * ROWS, c0 : c0 + w],
                0,
                0,
            ).astype(BF)
            for g in range(64):
                o_z, o_yhi, o_x, o_c = g // 16, (g // 8) % 2, (g // 2) % 4, g % 2
                i1, i2, i3 = spot(k, o_ylo, o_z, o_yhi, o_x)
                T[o_c, i1, i2, i3, :, 0:w] = half[g * 16 : g * 16 + 16, :]

    def head_product(k):
        T = s[f"T{k}"]
        grad = dot(s["grecv"][...].reshape(LATD * ROWS, OUTC), s["hidden"][...], 0, 0).astype(BF)
        for t in range(128):
            i1, i2, i3 = spot(k, t // 64, (t // 16) % 4, (t // 8) % 2, (t // 2) % 4)
            rt, ct = t // 5, t % 5
            if t < HEAD_TILES:
                T[t % 2, i1, i2, i3] = grad[rt * 16 : rt * 16 + 16, ct * 128 : ct * 128 + 128]
            else:
                T[t % 2, i1, i2, i3] = jnp.zeros((16, 128), BF)

    def stage1(k):
        a1 = at[order(k)[0]]
        T, Ra, Sb = s[f"T{k}"], s[f"Ra{k}"], s[f"Sb{k}"]
        rs_copy(k, 0).wait_recv()
        for j in (1, 2, 3):
            n = (a1 + j) % 4
            Sb[j - 1] = (T[core, n].astype(F32) + Ra[n].astype(F32)).astype(BF)
            rs_copy(k, 1, j).start()

    def stage2(k):
        a1, a2 = at[order(k)[0]], at[order(k)[1]]
        T, Ra, Rb, Sc = s[f"T{k}"], s[f"Ra{k}"], s[f"Rb{k}"], s[f"Sc{k}"]
        for j in (1, 2, 3):
            rs_copy(k, 1, j).wait_recv()
        for j in (1, 2, 3, 4):
            n = (a2 + j) % 4
            total = T[core, a1, n].astype(F32) + Ra[a1, n].astype(F32)
            for i in range(3):
                total = total + Rb[i, n].astype(F32)
            if j < 4:
                Sc[j - 1] = total.astype(BF)
                rs_copy(k, 2, j).start()
            else:
                s[f"Oc{k}"][...] = total

    def stage3(k):
        a3 = at[order(k)[2]]
        Oc, Rc, Sd = s[f"Oc{k}"], s[f"Rc{k}"], s[f"Sd{k}"]
        for j in (1, 2, 3):
            rs_copy(k, 2, j).wait_recv()
        for j in (1, 2, 3, 4):
            n = (a3 + j) % 4
            total = Oc[n]
            for i in range(3):
                total = total + Rc[i, n].astype(F32)
            Sd[j - 1] = total
            if j < 4:
                rs_copy(k, 3, j).start()

    def finish(k):
        name, c0, w, _ = CHUNKS[k]
        Sd, Rd = s[f"Sd{k}"], s[f"Rd{k}"]
        for j in (1, 2, 3):
            rs_copy(k, 3, j).wait_recv()
        total = Sd[3] + Rd[0] + Rd[1] + Rd[2]
        if name == "head":
            hall[core, h1, h2, h3] = total.astype(BF)
        else:
            out = s["o_gdn"] if name == "down" else s["o_gin"]
            out[:, c0 : c0 + w] = total[0:15, :]

    hall = s["hall"]
    h1, h2, h3 = (at[a] for a in order(0))

    def ag_copy(n, j=1):
        part = [hall.at[core, h1, h2, h3], hall.at[core, h1, h2], hall.at[core, h1], hall.at[core]][n]
        dev = partner("c", 1) if n == 3 else partner(order(0)[2 - n], j)
        m = 9 if n == 3 else 3 * n + j - 1
        return remote(part, part, s["ag_ss"].at[m], s["ag_rs"].at[m], dev)

    def ag_start(n):
        for j in (1,) if n == 3 else (1, 2, 3):
            ag_copy(n, j).start()

    def ag_wait(n):
        for j in (1,) if n == 3 else (1, 2, 3):
            ag_copy(n, j).wait_recv()

    def ar_copy(n, j=1):
        axis = "cxyz"[n]
        buf = s["ar" + axis]
        m = 0 if n == 0 else 3 * n - 3 + j
        part = buf.at[at[axis]]
        return remote(part, part, s["ar_ss"].at[m], s["ar_rs"].at[m], partner(axis, j))

    def ar_start(n, value):
        axis = "cxyz"[n]
        s["ar" + axis][at[axis]] = value
        for j in (1,) if n == 0 else (1, 2, 3):
            ar_copy(n, j).start()

    def ar_sum(n):
        buf = s["ar" + "cxyz"[n]]
        for j in (1,) if n == 0 else (1, 2, 3):
            ar_copy(n, j).wait_recv()
        total = buf[0]
        for i in range(1, 2 if n == 0 else 4):
            total = total + buf[i]
        return total

    def grad_hidden(ci, n):
        rows = pl.ds(pl.multiple_of(ci * ROWS, ROWS), n * ROWS)
        for i in range(n):
            for k in range(7):
                g_copy(ci + i, k).wait_recv()
        s["ghid"][rows, :] = dot(
            s["grecv"][pl.ds(ci, n)].reshape(n * ROWS, OUTC), s["whd"][...], 1, 0
        ).astype(BF)

    def grad_act(ci, n):
        rows = pl.ds(pl.multiple_of(ci * ROWS, ROWS), n * ROWS)
        ghid = s["ghid"][rows, :]
        for f in range(4):
            cols = slice(f * 512, f * 512 + 512)
            gact = dot(ghid, s["wdn"][cols, :], 1, 1)
            s["gpre"][rows, cols] = (s["slope"][rows, cols] * gact).astype(BF)

    def grad_normed(ci, n):
        rows = pl.ds(pl.multiple_of(ci * ROWS, ROWS), n * ROWS)
        s["cbuf"][0 : n * ROWS, :] = dot(s["gpre"][rows, :], s["win"][...], 1, 0)

    def conv_back(ci, r0):
        i = (ci + 1) % LATD
        gain_acc = jnp.zeros((8, D), F32)
        for q in range(ROWS // 32):
            here = slice(q * 32, q * 32 + 32)
            there = slice(r0 + q * 32, r0 + q * 32 + 32)
            gn = s["cbuf"][there, :]
            normal = s["normal"][ci, here, :]
            inv = s["istd"][ci, here, 0:1]
            gain_acc = gain_acc + jnp.sum((gn * normal).reshape(4, 8, D), axis=0)
            g = gn * gain
            s["cbuf"][there, :] = (
                g
                - jnp.mean(g, axis=-1, keepdims=True)
                - normal * jnp.mean(g * normal, axis=-1, keepdims=True)
            ) * inv
        s["cacc"][9] = s["cacc"][9] + gain_acc
        for lt in range(D // 128):
            lanes = slice(lt * 128, lt * 128 + 128)
            acc = [s["cacc"][n, :, lanes] for n in range(9)]
            for m in range(MEM):
                g1 = s["cbuf"][r0 + m * LON : r0 + (m + 1) * LON, lanes]
                moved = [pltpu.roll(g1, LON - 1, 0), g1, pltpu.roll(g1, 1, 0)]
                for a in range(3):
                    cells = mixed[i + a, m, :, lanes].astype(F32)
                    for b in range(3):
                        acc[3 * a + b] = acc[3 * a + b] + jnp.sum(
                            (cells * moved[b]).reshape(16, 8, 128), axis=0
                        )
            for n in range(9):
                s["cacc"][n, :, lanes] = acc[n]

    @pl.loop(0, 3)
    def _(ci):
        @pl.when(ci == 2)
        def _():
            score(LATD - 1)

        grad_hidden(ci, 1)
        grad_act(ci, 1)
        grad_normed(ci, 1)
        conv_back(ci, 0)

    def send0(k):
        rs_copy(k, 0).start()

    def sent(*stages):
        for k in range(7):
            for stage in stages:
                for j in (1,) if stage == 0 else (1, 2, 3):
                    rs_copy(k, stage, j).wait_send()

    activ, ghid, gpre, normed = s["activ"], s["ghid"], s["gpre"], s["normed"]
    grad_hidden(3, 1)
    head_product(0)
    send0(0)
    product(1, activ, ghid)
    send0(1)
    stage1(0)
    product(2, activ, ghid)
    send0(2)
    stage1(1)
    product(3, activ, ghid)
    send0(3)
    stage1(2)
    grad_act(3, 1)
    stage1(3)
    stage2(0)
    product(4, gpre, normed)
    send0(4)
    product(5, gpre, normed)
    send0(5)
    stage1(4)
    stage3(0)
    grad_normed(3, 1)
    stage1(5)
    stage2(1)
    conv_back(3, 0)
    ar_start(0, jnp.sum(s["cacc"][...], axis=1))
    product(6, gpre, normed)
    send0(6)
    ar_start(1, ar_sum(0))
    stage2(2)
    stage2(3)
    finish(0)
    ag_start(0)
    stage1(6)

    @pl.loop(0, LATD)
    def _(ci):
        for k in range(7):
            y_copy(ci, k).wait_send()
            g_copy(ci, k).wait_send()

    stage3(1)
    ag_wait(0)
    ag_start(1)
    sent(0, 1)
    stage2(4)
    ar_start(2, ar_sum(1))
    stage3(3)
    stage3(2)
    stage2(5)
    ag_wait(1)
    ag_start(2)
    stage2(6)
    finish(1)
    finish(3)
    finish(2)
    out_cp[1].start()
    sent(2)
    stage3(4)
    ar_start(3, ar_sum(2))
    stage3(6)
    stage3(5)
    ag_wait(2)
    ag_start(3)
    finish(4)
    finish(6)
    finish(5)
    out_cp[0].start()
    ag_wait(3)
    for t in range(HEAD_TILES):
        i1, i2, i3 = spot(0, t // 64, (t // 16) % 4, (t // 8) % 2, (t // 2) % 4)
        rt, ct = t // 5, t % 5
        s["o_head"][rt * 16 : rt * 16 + 16, ct * 128 : ct * 128 + 128] = hall[t % 2, i1, i2, i3].astype(F32)

    out_cp[2].start()
    sums = ar_sum(3)
    s["o_conv"][...] = sums[0:9]
    s["o_gain"][...] = sums[9, :]
    out_cp[3].start()
    out_cp[4].start()

    sent(3)
    for n in range(4):
        for j in (1,) if n == 3 else (1, 2, 3):
            ag_copy(n, j).wait_send()
        for j in (1,) if n == 0 else (1, 2, 3):
            ar_copy(n, j).wait_send()
    for cp in out_cp:
        cp.wait()


def hand_on(*refs):
    for k in range(5):
        refs[5 + k][...] = refs[k][...]


def body(
    latent_state, member_noise, conv_weight, norm_gain, weight_in, weight_down, weight_head, target_field
):
    vmem = pl.BlockSpec(memory_space=pltpu.VMEM)
    hbm = pl.BlockSpec(memory_space=pl.ANY)
    parts = pl.pallas_call(
        kernel,
        name="ensemble_block",
        out_shape=(
            jax.ShapeDtypeStruct((15, D), F32),
            jax.ShapeDtypeStruct((15, D), F32),
            jax.ShapeDtypeStruct((OUTC, D), F32),
            jax.ShapeDtypeStruct((D,), F32),
            jax.ShapeDtypeStruct((9, D), F32),
        ),
        in_specs=[hbm] * 8,
        out_specs=(hbm,) * 5,
        scratch_shapes=list(scratch().values()),
        compiler_params=pltpu.CompilerParams(
            collective_id=0, has_side_effects=True, vmem_limit_bytes=62 * 2**20
        ),
        cost_estimate=pl.CostEstimate(
            flops=17_000_000_000, bytes_accessed=9_000_000, transcendentals=2_100_000
        ),
    )(
        latent_state, member_noise, conv_weight, norm_gain, weight_in, weight_down,
        weight_head.T, jnp.swapaxes(target_field, 1, 2),
    )
    gin, gdn, head, gain, conv = pl.pallas_call(
        hand_on,
        name="hand_on",
        out_shape=(
            jax.ShapeDtypeStruct((15, D), F32),
            jax.ShapeDtypeStruct((15, D), F32),
            jax.ShapeDtypeStruct((OUTC, D), F32),
            jax.ShapeDtypeStruct((D,), F32),
            jax.ShapeDtypeStruct((9, D), F32),
        ),
        in_specs=[vmem] * 5,
        out_specs=(vmem,) * 5,
        cost_estimate=pl.CostEstimate(flops=0, bytes_accessed=1_900_000, transcendentals=0),
    )(*parts)
    return gin, gdn, head.T, gain, conv


def solution(mesh):
    return jax.shard_map(
        body,
        mesh=mesh,
        in_specs=(
            P("space", None, None),
            P("member", "space", None, None),
            P(),
            P(),
            P(),
            P(),
            P(),
            P("space", None, None),
        ),
        out_specs=(P(("member", "space"), None), P(("member", "space"), None), P(), P(), P()),
        check_vma=False,
    )
```

```python
import functools
import math

import jax
import jax.numpy as jnp
from jax import lax
from jax.experimental import pallas as pl
from jax.experimental.pallas import tpu as pltpu
from jax.sharding import PartitionSpec as P

BF = jnp.bfloat16
F32 = jnp.float32
MESH = pl.DeviceIdType.MESH

MEM = 2
LATD = 4
LON = 128
D = 640
OUTC = 320
FFR = 1920
FF = 2048
ROWS = MEM * LON
MEMBERS = 16
POINTS = 8192
SCALE = math.sqrt(MEMBERS * OUTC / POINTS)
GC = math.sqrt(2.0 / math.pi)
GROUP = [(dz, dy) for dz in range(4) for dy in range(2)][1:]
CHUNKS = [
    ("head", 0, 128, "zxy"),
    ("down", 0, 256, "xyz"),
    ("down", 256, 256, "yzx"),
    ("down", 512, 128, "zxy"),
    ("in", 0, 256, "xyz"),
    ("in", 256, 256, "yzx"),
    ("in", 512, 128, "zxy"),
]
HEAD_TILES = 100


def dot(a, b, ca, cb):
    return lax.dot_general(a, b, (((ca,), (cb,)), ((), ())), preferred_element_type=F32)


def scratch():
    out = {
        "win": pltpu.VMEM((FF, D), BF),
        "wdn": pltpu.VMEM((FF, D), BF),
        "whd": pltpu.VMEM((OUTC, D), BF),
        "tgt": pltpu.VMEM((LATD, LON, OUTC), F32),
        "mixed": pltpu.VMEM((LATD + 2, MEM, LON, D), BF),
        "cbuf": pltpu.VMEM((2 * ROWS, D), F32),
        "normal": pltpu.VMEM((LATD + 1, ROWS, D), F32),
        "istd": pltpu.VMEM((LATD + 1, ROWS, 128), F32),
        "normed": pltpu.VMEM(((LATD + 1) * ROWS, D), BF),
        "slope": pltpu.VMEM((LATD * ROWS, FF), F32),
        "activ": pltpu.VMEM((LATD * ROWS, FF), BF),
        "gpre": pltpu.VMEM((LATD * ROWS, FF), BF),
        "hidden": pltpu.VMEM((LATD * ROWS, D), BF),
        "ghid": pltpu.VMEM((LATD * ROWS, D), BF),
        "ysend": pltpu.VMEM((LATD, MEM, LON, OUTC), BF),
        "yrecv": pltpu.VMEM((LATD, MEMBERS, 16, OUTC), BF),
        "gsend": pltpu.VMEM((LATD, MEMBERS, 16, OUTC), BF),
        "grecv": pltpu.VMEM((LATD, MEM, LON, OUTC), BF),
        "cacc": pltpu.VMEM((10, 8, D), F32),
        "hall": pltpu.VMEM((2, 4, 4, 4, 16, 128), BF),
        "arc": pltpu.VMEM((2, 10, D), F32),
        "arx": pltpu.VMEM((4, 10, D), F32),
        "ary": pltpu.VMEM((4, 10, D), F32),
        "arz": pltpu.VMEM((4, 10, D), F32),
        "cw": pltpu.VMEM((9, D), F32),
        "gain": pltpu.VMEM((D,), F32),
        "o_gin": pltpu.VMEM((15, D), F32),
        "o_gdn": pltpu.VMEM((15, D), F32),
        "o_gain": pltpu.VMEM((D,), F32),
        "o_conv": pltpu.VMEM((9, D), F32),
        "o_sem": pltpu.SemaphoreType.DMA((5,)),
        "l_sem": pltpu.SemaphoreType.DMA((LATD + 3,)),
        "i_sem": pltpu.SemaphoreType.DMA((LATD, MEM + 1)),
        "w_sem": pltpu.SemaphoreType.DMA((2, 8)),
        "h_ss": pltpu.SemaphoreType.DMA((2,)),
        "h_rs": pltpu.SemaphoreType.DMA((2,)),
        "y_ss": pltpu.SemaphoreType.DMA((LATD, 7)),
        "y_rs": pltpu.SemaphoreType.DMA((LATD, 7)),
        "g_ss": pltpu.SemaphoreType.DMA((LATD, 7)),
        "g_rs": pltpu.SemaphoreType.DMA((LATD, 7)),
        "r_ss": pltpu.SemaphoreType.DMA((7, 10)),
        "r_rs": pltpu.SemaphoreType.DMA((7, 10)),
        "ag_ss": pltpu.SemaphoreType.DMA((10,)),
        "ag_rs": pltpu.SemaphoreType.DMA((10,)),
        "ar_ss": pltpu.SemaphoreType.DMA((10,)),
        "ar_rs": pltpu.SemaphoreType.DMA((10,)),
    }
    for k, (_, _, w, _) in enumerate(CHUNKS):
        out[f"T{k}"] = pltpu.VMEM((2, 4, 4, 4, 16, w), BF)
        out[f"Ra{k}"] = pltpu.VMEM((4, 4, 4, 16, w), BF)
        out[f"Sb{k}"] = pltpu.VMEM((3, 4, 4, 16, w), BF)
        out[f"Rb{k}"] = pltpu.VMEM((3, 4, 4, 16, w), BF)
        out[f"Sc{k}"] = pltpu.VMEM((3, 4, 16, w), BF)
        out[f"Oc{k}"] = pltpu.VMEM((4, 16, w), F32)
        out[f"Rc{k}"] = pltpu.VMEM((3, 4, 16, w), BF)
        out[f"Sd{k}"] = pltpu.VMEM((4, 16, w), F32)
        out[f"Rd{k}"] = pltpu.VMEM((3, 16, w), F32)
    return out


NAMES = list(scratch())


def kernel(
    lat_hbm, noise_hbm, cw_hbm, gain_hbm, win_hbm, wdn_hbm, whd_hbm, tgt_hbm,
    gin_hbm, gdn_hbm, head_hbm, ggain_hbm, gconv_hbm, *refs,
):
    s = dict(zip(NAMES, refs))
    member = lax.axis_index("member")
    space = lax.axis_index("space")
    ylo, z = member // 4, member % 4
    yhi, x, core = space // 8, (space // 2) % 4, space % 2
    y = yhi * 2 + ylo
    at = {"x": x, "y": y, "z": z, "c": core}

    def place(x_, y_, z_, c_):
        return ((y_ % 2) * 4 + z_, (y_ // 2) * 8 + x_ * 2 + c_)

    def partner(axis, step):
        c = dict(at)
        size = 2 if axis == "c" else 4
        c[axis] = (c[axis] + step) % size
        return place(c["x"], c["y"], c["z"], c["c"])

    def mate(dz, dy):
        return ((ylo + dy) % 2) * 4 + (z + dz) % 4

    def halo(step):
        return (member, (space + step) % 16)

    def remote(src, dst, ss, rs, dev):
        return pltpu.make_async_remote_copy(
            src_ref=src, dst_ref=dst, send_sem=ss, recv_sem=rs, device_id=dev, device_id_type=MESH
        )

    barrier = pltpu.get_barrier_semaphore()
    friends = [(mate(dz, dy), space) for dz, dy in GROUP]
    friends += [partner("c", 1), halo(1), halo(-1)]
    friends += [partner(a, j) for a in "xy" for j in (1, 2, 3)]
    for dev in friends:
        pl.semaphore_signal(barrier, inc=1, device_id=dev, device_id_type=MESH)

    lsem = s["l_sem"]

    def cells_raw(i, m):
        n = (i * MEM + m) * LON
        return s["hidden"].at[n : n + LON]

    def latent_raw(i):
        return s["ghid"].at[i * LON : i * LON + LON]

    cells_cp = [
        [
            pltpu.make_async_copy(noise_hbm.at[m, i], cells_raw(i, m), s["i_sem"].at[i, m])
            for m in range(MEM)
        ]
        + [pltpu.make_async_copy(lat_hbm.at[i], latent_raw(i), s["i_sem"].at[i, MEM])]
        for i in range(LATD)
    ]

    def raw(name, b):
        r, c = (b % 4) * 240, (b // 4) * D
        return s[name].at[r : r + 240, c : c + D]

    win_cp = [
        pltpu.make_async_copy(win_hbm.at[240 * b : 240 * b + 240], raw("activ", b), s["w_sem"].at[0, b])
        for b in range(8)
    ]
    wdn_cp = [
        pltpu.make_async_copy(wdn_hbm.at[240 * b : 240 * b + 240], raw("gpre", b), s["w_sem"].at[1, b])
        for b in range(8)
    ]
    whd_cp = pltpu.make_async_copy(whd_hbm, s["whd"], lsem.at[LATD])

    def traw(i):
        return s["slope"].at[0:OUTC, LON * i : LON * i + LON]

    tgt_cp = [
        pltpu.make_async_copy(tgt_hbm.at[i], traw(i), lsem.at[i]) for i in range(LATD)
    ]
    cw_cp = pltpu.make_async_copy(cw_hbm, s["cw"], lsem.at[LATD + 1])
    gain_cp = pltpu.make_async_copy(gain_hbm, s["gain"], lsem.at[LATD + 2])
    out_cp = [
        pltpu.make_async_copy(s[n], dst, s["o_sem"].at[k])
        for k, (n, dst) in enumerate(
            (
                ("o_gin", gin_hbm),
                ("o_gdn", gdn_hbm),
                ("hall", head_hbm),
                ("o_gain", ggain_hbm),
                ("o_conv", gconv_hbm),
            )
        )
    ]
    mine16 = pl.ds(pl.multiple_of(member * 16, 16), 16)
    for i in (0, 3, 1, 2):
        for cp in cells_cp[i]:
            cp.start()
    for cp in (cw_cp, gain_cp, *win_cp, *wdn_cp, whd_cp, *tgt_cp):
        cp.start()

    mixed = s["mixed"]

    def mix(i):
        for cp in cells_cp[i]:
            cp.wait()
        base = latent_raw(i)[...].astype(F32)
        for m in range(MEM):
            mixed[i + 1, m] = (base + cells_raw(i, m)[...].astype(F32)).astype(BF)

    halo_cp = [
        remote(mixed.at[1], mixed.at[5], s["h_ss"].at[0], s["h_rs"].at[0], halo(-1)),
        remote(mixed.at[4], mixed.at[0], s["h_ss"].at[1], s["h_rs"].at[1], halo(1)),
    ]
    mix(0)
    mix(3)
    pl.semaphore_wait(barrier, len(friends))
    for cp in halo_cp:
        cp.start()
    mix(1)
    mix(2)

    row_at = lax.broadcasted_iota(jnp.int32, (256, 240), 0)
    col_at = lax.broadcasted_iota(jnp.int32, (256, 240), 1)
    spread = jnp.where(
        (row_at % 16 < 15) & (col_at == (row_at // 16) * 15 + row_at % 16), 1.0, 0.0
    ).astype(BF)

    def pad_rows(dst, name):
        for b in range(8):
            r, c = (b % 4) * 240, (b // 4) * D
            dst[256 * b : 256 * b + 256, :] = dot(
                spread, s[name][r : r + 240, c : c + D], 1, 0
            ).astype(BF)

    def y_copy(ci, k):
        dz, dy = GROUP[k]
        to = mate(dz, dy)
        return remote(
            s["ysend"].at[ci, :, pl.ds(pl.multiple_of(to * 16, 16), 16)],
            s["yrecv"].at[ci, pl.ds(member * 2, 2)],
            s["y_ss"].at[ci, k], s["y_rs"].at[ci, k], (to, space),
        )

    def g_copy(ci, k):
        dz, dy = GROUP[k]
        to = mate(dz, dy)
        return remote(
            s["gsend"].at[ci, pl.ds(to * 2, 2)],
            s["grecv"].at[ci, :, mine16],
            s["g_ss"].at[ci, k], s["g_rs"].at[ci, k], (to, space),
        )


    def conv_norm(ci):
        i = (ci + 1) % LATD
        r0 = pl.multiple_of(ci * ROWS, ROWS)
        for m in range(MEM):
            for lt in range(D // 128):
                lanes = slice(lt * 128, lt * 128 + 128)
                part = [None] * 3
                for a in range(3):
                    cells = mixed[i + a, m, :, lanes].astype(F32)
                    for b in range(3):
                        term = s["cw"][3 * a + b : 3 * a + b + 1, lanes] * cells
                        part[b] = term if a == 0 else part[b] + term
                s["cbuf"][m * LON : (m + 1) * LON, lanes] = (
                    part[1] + pltpu.roll(part[0], 1, 0) + pltpu.roll(part[2], LON - 1, 0)
                )
        for q in range(ROWS // 32):
            here = slice(q * 32, q * 32 + 32)
            conv = s["cbuf"][here, :]
            center = conv - jnp.mean(conv, axis=-1, keepdims=True)
            inv = lax.rsqrt(jnp.mean(center * center, axis=-1, keepdims=True) + 1e-05)
            normal = center * inv
            s["normal"][ci, here, :] = normal
            s["istd"][ci, here, :] = jnp.broadcast_to(inv, (32, 128))
            s["normed"][pl.ds(pl.multiple_of(r0 + q * 32, 32), 32), :] = (normal * gain).astype(BF)

    def mixer(ci):
        i = (ci + 1) % LATD
        rows = pl.ds(pl.multiple_of(ci * ROWS, ROWS), ROWS)
        normed = s["normed"][rows, :]
        for f in range(4):
            cols = slice(f * 512, f * 512 + 512)
            pre = dot(normed, s["win"][cols, :], 1, 1)
            sq = pre * pre
            t = jnp.tanh(pre * (GC + (GC * 0.044715) * sq))
            half = 0.5 + 0.5 * t
            act = pre * half
            s["activ"][rows, cols] = act.astype(BF)
            s["slope"][rows, cols] = half + act * (1.0 - t) * (GC + (3 * GC * 0.044715) * sq)
        down = dot(s["activ"][rows, :], s["wdn"][...], 1, 0)
        base = mixed[i + 1].reshape(ROWS, D).astype(F32)
        hidden = (base + down).astype(BF)
        s["hidden"][rows, :] = hidden
        pred = dot(hidden, s["whd"][...], 1, 1)
        s["ysend"][ci] = pred.astype(BF).reshape(MEM, LON, OUTC)
        s["yrecv"][ci, pl.ds(member * 2, 2)] = s["ysend"][ci, :, mine16]

    def score(ci):
        i = (ci + 1) % LATD
        for k in range(7):
            y_copy(ci, k).wait_recv()
        yb = s["yrecv"][ci].reshape(256, OUTC)
        gram = dot(yb, yb, 1, 1)
        r = lax.broadcasted_iota(jnp.int32, (256, 256), 0)
        c = lax.broadcasted_iota(jnp.int32, (256, 256), 1)
        diag = jnp.where(r == c, gram, 0.0)
        sq_r = jnp.sum(diag, axis=1, keepdims=True)
        sq_c = jnp.sum(diag, axis=0, keepdims=True)
        inv = lax.rsqrt(jnp.maximum(sq_r + sq_c - 2.0 * gram + 1.0, 1.0))
        w = jnp.where(r % 16 == c % 16, inv, 0.0).astype(BF)
        w_sum = jnp.sum(w.astype(F32), axis=1, keepdims=True)
        pulled = dot(w, yb, 1, 0)
        yf = yb.astype(F32)
        err = (yf.reshape(16, 16, OUTC) - s["tgt"][i, mine16, :][None]).reshape(256, OUTC)
        far = lax.rsqrt(jnp.sum(err * err, axis=-1, keepdims=True) + 1.0)
        grad = err * (far * (SCALE / MEMBERS)) - (yf * w_sum - pulled) * (
            SCALE / (MEMBERS * (MEMBERS - 1))
        )
        s["gsend"][ci] = grad.astype(BF).reshape(MEMBERS, 16, OUTC)
        s["grecv"][ci, :, mine16] = s["gsend"][ci, pl.ds(member * 2, 2)]
        for k in range(7):
            g_copy(ci, k).start()

    for cp in (cw_cp, gain_cp):
        cp.wait()
    s["cacc"][...] = jnp.zeros((10, 8, D), F32)
    gain = s["gain"][...].reshape(1, D)
    conv_norm(0)
    for cp in (*win_cp, *wdn_cp, whd_cp, *tgt_cp):
        cp.wait()
    pad_rows(s["win"], "activ")
    pad_rows(s["wdn"], "gpre")
    for i in range(LATD):
        s["tgt"][i] = traw(i)[...].T

    @pl.loop(0, LATD)
    def _(ci):
        @pl.when(ci == 1)
        def _():
            for cp in halo_cp:
                cp.wait()

            @pl.when(space == 0)
            def _():
                mixed[0] = jnp.zeros((MEM, LON, D), BF)

            @pl.when(space == 15)
            def _():
                mixed[5] = jnp.zeros((MEM, LON, D), BF)

        mixer(ci)
        conv_norm(ci + 1)
        for k in range(7):
            y_copy(ci, k).start()

        @pl.when(ci > 1)
        def _():
            score(ci - 2)

    def order(k):
        return CHUNKS[k][3]

    def rs_copy(k, stage, j=1):
        o = order(k)
        if stage == 0:
            n, src, dst, dev = 0, s[f"T{k}"].at[1 - core], s[f"Ra{k}"], partner("c", 1)
        else:
            pair = {1: ("Sb", "Rb"), 2: ("Sc", "Rc"), 3: ("Sd", "Rd")}[stage]
            n = 3 * (stage - 1) + j
            src, dst = s[f"{pair[0]}{k}"].at[j - 1], s[f"{pair[1]}{k}"].at[j - 1]
            dev = partner(o[stage - 1], j)
        return remote(src, dst, s["r_ss"].at[k, n], s["r_rs"].at[k, n], dev)

    def spot(k, o_ylo, o_z, o_yhi, o_x):
        v = {"x": o_x, "y": o_yhi * 2 + o_ylo, "z": o_z}
        return tuple(v[a] for a in order(k))

    def product(k, left, right):
        _, c0, w, _ = CHUNKS[k]
        T = s[f"T{k}"]

        @pl.loop(0, 2)
        def _(o_ylo):
            half = dot(
                left[:, pl.ds(pl.multiple_of(o_ylo * 1024, 1024), 1024)],
                right[0 : LATD * ROWS, c0 : c0 + w],
                0,
                0,
            ).astype(BF)
            for g in range(64):
                o_z, o_yhi, o_x, o_c = g // 16, (g // 8) % 2, (g // 2) % 4, g % 2
                i1, i2, i3 = spot(k, o_ylo, o_z, o_yhi, o_x)
                T[o_c, i1, i2, i3, :, 0:w] = half[g * 16 : g * 16 + 16, :]

    def head_product(k):
        T = s[f"T{k}"]
        grad = dot(s["grecv"][...].reshape(LATD * ROWS, OUTC), s["hidden"][...], 0, 0).astype(BF)
        for t in range(128):
            i1, i2, i3 = spot(k, t // 64, (t // 16) % 4, (t // 8) % 2, (t // 2) % 4)
            rt, ct = t // 5, t % 5
            if t < HEAD_TILES:
                T[t % 2, i1, i2, i3] = grad[rt * 16 : rt * 16 + 16, ct * 128 : ct * 128 + 128]
            else:
                T[t % 2, i1, i2, i3] = jnp.zeros((16, 128), BF)

    def stage1(k):
        a1 = at[order(k)[0]]
        T, Ra, Sb = s[f"T{k}"], s[f"Ra{k}"], s[f"Sb{k}"]
        rs_copy(k, 0).wait_recv()
        for j in (1, 2, 3):
            n = (a1 + j) % 4
            Sb[j - 1] = (T[core, n].astype(F32) + Ra[n].astype(F32)).astype(BF)
            rs_copy(k, 1, j).start()

    def stage2(k):
        a1, a2 = at[order(k)[0]], at[order(k)[1]]
        T, Ra, Rb, Sc = s[f"T{k}"], s[f"Ra{k}"], s[f"Rb{k}"], s[f"Sc{k}"]
        for j in (1, 2, 3):
            rs_copy(k, 1, j).wait_recv()
        for j in (1, 2, 3, 4):
            n = (a2 + j) % 4
            total = T[core, a1, n].astype(F32) + Ra[a1, n].astype(F32)
            for i in range(3):
                total = total + Rb[i, n].astype(F32)
            if j < 4:
                Sc[j - 1] = total.astype(BF)
                rs_copy(k, 2, j).start()
            else:
                s[f"Oc{k}"][...] = total

    def stage3(k):
        a3 = at[order(k)[2]]
        Oc, Rc, Sd = s[f"Oc{k}"], s[f"Rc{k}"], s[f"Sd{k}"]
        for j in (1, 2, 3):
            rs_copy(k, 2, j).wait_recv()
        for j in (1, 2, 3, 4):
            n = (a3 + j) % 4
            total = Oc[n]
            for i in range(3):
                total = total + Rc[i, n].astype(F32)
            Sd[j - 1] = total
            if j < 4:
                rs_copy(k, 3, j).start()

    def finish(k):
        name, c0, w, _ = CHUNKS[k]
        Sd, Rd = s[f"Sd{k}"], s[f"Rd{k}"]
        for j in (1, 2, 3):
            rs_copy(k, 3, j).wait_recv()
        total = Sd[3] + Rd[0] + Rd[1] + Rd[2]
        if name == "head":
            hall[core, h1, h2, h3] = total.astype(BF)
        else:
            out = s["o_gdn"] if name == "down" else s["o_gin"]
            out[:, c0 : c0 + w] = total[0:15, :]

    hall = s["hall"]
    h1, h2, h3 = (at[a] for a in order(0))

    def ag_copy(n, j=1):
        part = [hall.at[core, h1, h2, h3], hall.at[core, h1, h2], hall.at[core, h1], hall.at[core]][n]
        dev = partner("c", 1) if n == 3 else partner(order(0)[2 - n], j)
        m = 9 if n == 3 else 3 * n + j - 1
        return remote(part, part, s["ag_ss"].at[m], s["ag_rs"].at[m], dev)

    def ag_start(n):
        for j in (1,) if n == 3 else (1, 2, 3):
            ag_copy(n, j).start()

    def ag_wait(n):
        for j in (1,) if n == 3 else (1, 2, 3):
            ag_copy(n, j).wait_recv()

    def ar_copy(n, j=1):
        axis = "cxyz"[n]
        buf = s["ar" + axis]
        m = 0 if n == 0 else 3 * n - 3 + j
        part = buf.at[at[axis]]
        return remote(part, part, s["ar_ss"].at[m], s["ar_rs"].at[m], partner(axis, j))

    def ar_start(n, value):
        axis = "cxyz"[n]
        s["ar" + axis][at[axis]] = value
        for j in (1,) if n == 0 else (1, 2, 3):
            ar_copy(n, j).start()

    def ar_sum(n):
        buf = s["ar" + "cxyz"[n]]
        for j in (1,) if n == 0 else (1, 2, 3):
            ar_copy(n, j).wait_recv()
        total = buf[0]
        for i in range(1, 2 if n == 0 else 4):
            total = total + buf[i]
        return total

    def grad_hidden(ci, n):
        rows = pl.ds(pl.multiple_of(ci * ROWS, ROWS), n * ROWS)
        for i in range(n):
            for k in range(7):
                g_copy(ci + i, k).wait_recv()
        s["ghid"][rows, :] = dot(
            s["grecv"][pl.ds(ci, n)].reshape(n * ROWS, OUTC), s["whd"][...], 1, 0
        ).astype(BF)

    def grad_act(ci, n):
        rows = pl.ds(pl.multiple_of(ci * ROWS, ROWS), n * ROWS)
        ghid = s["ghid"][rows, :]
        for f in range(4):
            cols = slice(f * 512, f * 512 + 512)
            gact = dot(ghid, s["wdn"][cols, :], 1, 1)
            s["gpre"][rows, cols] = (s["slope"][rows, cols] * gact).astype(BF)

    def grad_normed(ci, n):
        rows = pl.ds(pl.multiple_of(ci * ROWS, ROWS), n * ROWS)
        s["cbuf"][0 : n * ROWS, :] = dot(s["gpre"][rows, :], s["win"][...], 1, 0)

    def conv_back(ci, r0):
        i = (ci + 1) % LATD
        gain_acc = jnp.zeros((8, D), F32)
        for q in range(ROWS // 32):
            here = slice(q * 32, q * 32 + 32)
            there = slice(r0 + q * 32, r0 + q * 32 + 32)
            gn = s["cbuf"][there, :]
            normal = s["normal"][ci, here, :]
            inv = s["istd"][ci, here, 0:1]
            gain_acc = gain_acc + jnp.sum((gn * normal).reshape(4, 8, D), axis=0)
            g = gn * gain
            s["cbuf"][there, :] = (
                g
                - jnp.mean(g, axis=-1, keepdims=True)
                - normal * jnp.mean(g * normal, axis=-1, keepdims=True)
            ) * inv
        s["cacc"][9] = s["cacc"][9] + gain_acc
        for lt in range(D // 128):
            lanes = slice(lt * 128, lt * 128 + 128)
            acc = [s["cacc"][n, :, lanes] for n in range(9)]
            for m in range(MEM):
                g1 = s["cbuf"][r0 + m * LON : r0 + (m + 1) * LON, lanes]
                moved = [pltpu.roll(g1, LON - 1, 0), g1, pltpu.roll(g1, 1, 0)]
                for a in range(3):
                    cells = mixed[i + a, m, :, lanes].astype(F32)
                    for b in range(3):
                        acc[3 * a + b] = acc[3 * a + b] + jnp.sum(
                            (cells * moved[b]).reshape(16, 8, 128), axis=0
                        )
            for n in range(9):
                s["cacc"][n, :, lanes] = acc[n]

    @pl.loop(0, 3)
    def _(ci):
        @pl.when(ci < 2)
        def _():
            score(ci + 2)

        grad_hidden(ci, 1)
        grad_act(ci, 1)
        grad_normed(ci, 1)
        conv_back(ci, 0)

    def send0(k):
        rs_copy(k, 0).start()

    def sent(*stages):
        for k in range(7):
            for stage in stages:
                for j in (1,) if stage == 0 else (1, 2, 3):
                    rs_copy(k, stage, j).wait_send()

    activ, ghid, gpre, normed = s["activ"], s["ghid"], s["gpre"], s["normed"]
    grad_hidden(3, 1)
    head_product(0)
    send0(0)
    product(1, activ, ghid)
    send0(1)
    stage1(0)
    product(2, activ, ghid)
    send0(2)
    stage1(1)
    product(3, activ, ghid)
    send0(3)
    stage1(2)
    grad_act(3, 1)
    stage1(3)
    product(4, gpre, normed)
    send0(4)
    stage2(0)
    product(5, gpre, normed)
    send0(5)
    stage1(4)
    product(6, gpre, normed)
    send0(6)
    stage1(5)
    stage3(0)
    grad_normed(3, 1)
    stage1(6)
    stage2(1)
    stage2(2)
    conv_back(3, 0)
    ar_start(0, jnp.sum(s["cacc"][...], axis=1))
    stage2(3)
    ar_start(1, ar_sum(0))
    finish(0)
    ag_start(0)

    @pl.loop(0, LATD)
    def _(ci):
        for k in range(7):
            y_copy(ci, k).wait_send()
            g_copy(ci, k).wait_send()

    stage3(1)
    stage3(2)
    ag_wait(0)
    ag_start(1)
    stage3(3)
    stage2(4)
    stage2(5)
    ar_start(2, ar_sum(1))
    stage2(6)
    ag_wait(1)
    ag_start(2)
    finish(1)
    finish(2)
    finish(3)
    out_cp[1].start()
    stage3(4)
    stage3(5)
    ar_start(3, ar_sum(2))
    stage3(6)
    ag_wait(2)
    ag_start(3)
    sent(0, 1)
    sent(2)
    finish(4)
    finish(5)
    finish(6)
    out_cp[0].start()
    ag_wait(3)
    out_cp[2].start()
    sums = ar_sum(3)
    s["o_conv"][...] = sums[0:9]
    s["o_gain"][...] = sums[9, :]
    out_cp[3].start()
    out_cp[4].start()

    sent(3)
    for n in range(4):
        for j in (1,) if n == 3 else (1, 2, 3):
            ag_copy(n, j).wait_send()
        for j in (1,) if n == 0 else (1, 2, 3):
            ar_copy(n, j).wait_send()
    for cp in out_cp:
        cp.wait()


def hand_on(gin, gdn, tiles, gain, conv, gin_out, gdn_out, head_out, gain_out, conv_out):
    gin_out[...] = gin[...]
    gdn_out[...] = gdn[...]
    for t in range(HEAD_TILES):
        v = {"x": (t // 2) % 4, "y": (t // 8) % 2 * 2 + t // 64, "z": (t // 16) % 4}
        i1, i2, i3 = (v[a] for a in CHUNKS[0][3])
        rt, ct = t // 5, t % 5
        head_out[rt * 16 : rt * 16 + 16, ct * 128 : ct * 128 + 128] = tiles[t % 2, i1, i2, i3].astype(F32)
    gain_out[...] = gain[...]
    conv_out[...] = conv[...]


def body(
    latent_state, member_noise, conv_weight, norm_gain, weight_in, weight_down, weight_head, target_field
):
    vmem = pl.BlockSpec(memory_space=pltpu.VMEM)
    hbm = pl.BlockSpec(memory_space=pl.ANY)
    parts = pl.pallas_call(
        kernel,
        name="ensemble_block",
        out_shape=(
            jax.ShapeDtypeStruct((15, D), F32),
            jax.ShapeDtypeStruct((15, D), F32),
            jax.ShapeDtypeStruct((2, 4, 4, 4, 16, 128), BF),
            jax.ShapeDtypeStruct((D,), F32),
            jax.ShapeDtypeStruct((9, D), F32),
        ),
        in_specs=[hbm] * 8,
        out_specs=(hbm,) * 5,
        scratch_shapes=list(scratch().values()),
        compiler_params=pltpu.CompilerParams(
            collective_id=0, has_side_effects=True, vmem_limit_bytes=62 * 2**20
        ),
        cost_estimate=pl.CostEstimate(
            flops=17_000_000_000, bytes_accessed=9_000_000, transcendentals=2_100_000
        ),
    )(
        latent_state, member_noise, conv_weight, norm_gain, weight_in, weight_down,
        weight_head.T, jnp.swapaxes(target_field, 1, 2),
    )
    gin, gdn, head, gain, conv = pl.pallas_call(
        hand_on,
        name="hand_on",
        out_shape=(
            jax.ShapeDtypeStruct((15, D), F32),
            jax.ShapeDtypeStruct((15, D), F32),
            jax.ShapeDtypeStruct((OUTC, D), F32),
            jax.ShapeDtypeStruct((D,), F32),
            jax.ShapeDtypeStruct((9, D), F32),
        ),
        in_specs=[vmem] * 5,
        out_specs=(vmem,) * 5,
        cost_estimate=pl.CostEstimate(flops=0, bytes_accessed=1_900_000, transcendentals=0),
    )(*parts)
    return gin, gdn, head.T, gain, conv


def solution(mesh):
    return jax.shard_map(
        body,
        mesh=mesh,
        in_specs=(
            P("space", None, None),
            P("member", "space", None, None),
            P(),
            P(),
            P(),
            P(),
            P(),
            P("space", None, None),
        ),
        out_specs=(P(("member", "space"), None), P(("member", "space"), None), P(), P(), P()),
        check_vma=False,
    )
```

```python
import functools
import math

import jax
import jax.numpy as jnp
from jax import lax
from jax.experimental import pallas as pl
from jax.experimental.pallas import tpu as pltpu
from jax.sharding import PartitionSpec as P

BF = jnp.bfloat16
F32 = jnp.float32
MESH = pl.DeviceIdType.MESH

MEM = 2
LATD = 4
LON = 128
D = 640
OUTC = 320
FFR = 1920
FF = 2048
ROWS = MEM * LON
MEMBERS = 16
POINTS = 8192
SCALE = math.sqrt(MEMBERS * OUTC / POINTS)
GC = math.sqrt(2.0 / math.pi)
GROUP = [(dz, dy) for dz in range(4) for dy in range(2)][1:]
CHUNKS = [
    ("head", 0, 128, "zxy"),
    ("down", 0, 256, "xyz"),
    ("down", 256, 256, "yzx"),
    ("down", 512, 128, "zxy"),
    ("in", 0, 256, "xyz"),
    ("in", 256, 256, "yzx"),
    ("in", 512, 128, "zxy"),
]
HEAD_TILES = 100


def dot(a, b, ca, cb):
    return lax.dot_general(a, b, (((ca,), (cb,)), ((), ())), preferred_element_type=F32)


def scratch():
    out = {
        "win": pltpu.VMEM((FF, D), BF),
        "wdn": pltpu.VMEM((FF, D), BF),
        "whd": pltpu.VMEM((OUTC, D), BF),
        "tgt": pltpu.VMEM((LATD, LON, OUTC), F32),
        "mixed": pltpu.VMEM((LATD + 2, MEM, LON, D), BF),
        "cbuf": pltpu.VMEM((2 * ROWS, D), F32),
        "normal": pltpu.VMEM((LATD + 1, ROWS, D), F32),
        "istd": pltpu.VMEM((LATD + 1, ROWS, 128), F32),
        "normed": pltpu.VMEM(((LATD + 1) * ROWS, D), BF),
        "slope": pltpu.VMEM((LATD * ROWS, FF), F32),
        "activ": pltpu.VMEM((LATD * ROWS, FF), BF),
        "gpre": pltpu.VMEM((LATD * ROWS, FF), BF),
        "hidden": pltpu.VMEM((LATD * ROWS, D), BF),
        "ghid": pltpu.VMEM((LATD * ROWS, D), BF),
        "ysend": pltpu.VMEM((LATD, MEM, LON, OUTC), BF),
        "yrecv": pltpu.VMEM((LATD, MEMBERS, 16, OUTC), BF),
        "gsend": pltpu.VMEM((LATD, MEMBERS, 16, OUTC), BF),
        "grecv": pltpu.VMEM((LATD, MEM, LON, OUTC), BF),
        "cacc": pltpu.VMEM((10, 8, D), F32),
        "hall": pltpu.VMEM((2, 4, 4, 4, 16, 128), BF),
        "arc": pltpu.VMEM((2, 10, D), F32),
        "arx": pltpu.VMEM((4, 10, D), F32),
        "ary": pltpu.VMEM((4, 10, D), F32),
        "arz": pltpu.VMEM((4, 10, D), F32),
        "cw": pltpu.VMEM((9, D), F32),
        "gain": pltpu.VMEM((D,), F32),
        "o_gin": pltpu.VMEM((15, D), F32),
        "o_gdn": pltpu.VMEM((15, D), F32),
        "o_gain": pltpu.VMEM((D,), F32),
        "o_conv": pltpu.VMEM((9, D), F32),
        "o_sem": pltpu.SemaphoreType.DMA((5,)),
        "l_sem": pltpu.SemaphoreType.DMA((LATD + 3,)),
        "i_sem": pltpu.SemaphoreType.DMA((LATD, MEM + 1)),
        "w_sem": pltpu.SemaphoreType.DMA((2, 8)),
        "h_ss": pltpu.SemaphoreType.DMA((2,)),
        "h_rs": pltpu.SemaphoreType.DMA((2,)),
        "y_ss": pltpu.SemaphoreType.DMA((LATD, 7)),
        "y_rs": pltpu.SemaphoreType.DMA((LATD, 7)),
        "g_ss": pltpu.SemaphoreType.DMA((LATD, 7)),
        "g_rs": pltpu.SemaphoreType.DMA((LATD, 7)),
        "r_ss": pltpu.SemaphoreType.DMA((7, 10)),
        "r_rs": pltpu.SemaphoreType.DMA((7, 10)),
        "ag_ss": pltpu.SemaphoreType.DMA((10,)),
        "ag_rs": pltpu.SemaphoreType.DMA((10,)),
        "ar_ss": pltpu.SemaphoreType.DMA((10,)),
        "ar_rs": pltpu.SemaphoreType.DMA((10,)),
    }
    for k, (_, _, w, _) in enumerate(CHUNKS):
        out[f"T{k}"] = pltpu.VMEM((2, 4, 4, 4, 16, w), BF)
        out[f"Ra{k}"] = pltpu.VMEM((4, 4, 4, 16, w), BF)
        out[f"Sb{k}"] = pltpu.VMEM((3, 4, 4, 16, w), BF)
        out[f"Rb{k}"] = pltpu.VMEM((3, 4, 4, 16, w), BF)
        out[f"Sc{k}"] = pltpu.VMEM((3, 4, 16, w), BF)
        out[f"Oc{k}"] = pltpu.VMEM((4, 16, w), F32)
        out[f"Rc{k}"] = pltpu.VMEM((3, 4, 16, w), BF)
        out[f"Sd{k}"] = pltpu.VMEM((4, 16, w), F32)
        out[f"Rd{k}"] = pltpu.VMEM((3, 16, w), F32)
    return out


NAMES = list(scratch())


def kernel(
    lat_hbm, noise_hbm, cw_hbm, gain_hbm, win_hbm, wdn_hbm, whd_hbm, tgt_hbm,
    gin_hbm, gdn_hbm, head_hbm, ggain_hbm, gconv_hbm, *refs,
):
    s = dict(zip(NAMES, refs))
    member = lax.axis_index("member")
    space = lax.axis_index("space")
    ylo, z = member // 4, member % 4
    yhi, x, core = space // 8, (space // 2) % 4, space % 2
    y = yhi * 2 + ylo
    at = {"x": x, "y": y, "z": z, "c": core}

    def place(x_, y_, z_, c_):
        return ((y_ % 2) * 4 + z_, (y_ // 2) * 8 + x_ * 2 + c_)

    def partner(axis, step):
        c = dict(at)
        size = 2 if axis == "c" else 4
        c[axis] = (c[axis] + step) % size
        return place(c["x"], c["y"], c["z"], c["c"])

    def mate(dz, dy):
        return ((ylo + dy) % 2) * 4 + (z + dz) % 4

    def halo(step):
        return (member, (space + step) % 16)

    def remote(src, dst, ss, rs, dev):
        return pltpu.make_async_remote_copy(
            src_ref=src, dst_ref=dst, send_sem=ss, recv_sem=rs, device_id=dev, device_id_type=MESH
        )

    barrier = pltpu.get_barrier_semaphore()
    friends = [(mate(dz, dy), space) for dz, dy in GROUP]
    friends += [partner("c", 1), halo(1), halo(-1)]
    friends += [partner(a, j) for a in "xy" for j in (1, 2, 3)]
    for dev in friends:
        pl.semaphore_signal(barrier, inc=1, device_id=dev, device_id_type=MESH)

    lsem = s["l_sem"]

    def cells_raw(i, m):
        n = (i * MEM + m) * LON
        return s["hidden"].at[n : n + LON]

    def latent_raw(i):
        return s["ghid"].at[i * LON : i * LON + LON]

    cells_cp = [
        [
            pltpu.make_async_copy(noise_hbm.at[m, i], cells_raw(i, m), s["i_sem"].at[i, m])
            for m in range(MEM)
        ]
        + [pltpu.make_async_copy(lat_hbm.at[i], latent_raw(i), s["i_sem"].at[i, MEM])]
        for i in range(LATD)
    ]

    def raw(name, b):
        r, c = (b % 4) * 240, (b // 4) * D
        return s[name].at[r : r + 240, c : c + D]

    win_cp = [
        pltpu.make_async_copy(win_hbm.at[240 * b : 240 * b + 240], raw("activ", b), s["w_sem"].at[0, b])
        for b in range(8)
    ]
    wdn_cp = [
        pltpu.make_async_copy(wdn_hbm.at[240 * b : 240 * b + 240], raw("gpre", b), s["w_sem"].at[1, b])
        for b in range(8)
    ]
    whd_cp = pltpu.make_async_copy(whd_hbm, s["whd"], lsem.at[LATD])

    def traw(i):
        return s["slope"].at[0:OUTC, LON * i : LON * i + LON]

    tgt_cp = [
        pltpu.make_async_copy(tgt_hbm.at[i], traw(i), lsem.at[i]) for i in range(LATD)
    ]
    cw_cp = pltpu.make_async_copy(cw_hbm, s["cw"], lsem.at[LATD + 1])
    gain_cp = pltpu.make_async_copy(gain_hbm, s["gain"], lsem.at[LATD + 2])
    out_cp = [
        pltpu.make_async_copy(s[n], dst, s["o_sem"].at[k])
        for k, (n, dst) in enumerate(
            (
                ("o_gin", gin_hbm),
                ("o_gdn", gdn_hbm),
                ("hall", head_hbm),
                ("o_gain", ggain_hbm),
                ("o_conv", gconv_hbm),
            )
        )
    ]
    mine16 = pl.ds(pl.multiple_of(member * 16, 16), 16)
    for i in (0, 3, 1, 2):
        for cp in cells_cp[i]:
            cp.start()
    for cp in (cw_cp, gain_cp, *win_cp, *wdn_cp, whd_cp, *tgt_cp):
        cp.start()

    mixed = s["mixed"]

    def mix(i):
        for cp in cells_cp[i]:
            cp.wait()
        base = latent_raw(i)[...].astype(F32)
        for m in range(MEM):
            mixed[i + 1, m] = (base + cells_raw(i, m)[...].astype(F32)).astype(BF)

    halo_cp = [
        remote(mixed.at[1], mixed.at[5], s["h_ss"].at[0], s["h_rs"].at[0], halo(-1)),
        remote(mixed.at[4], mixed.at[0], s["h_ss"].at[1], s["h_rs"].at[1], halo(1)),
    ]
    mix(0)
    mix(3)
    pl.semaphore_wait(barrier, len(friends))
    for cp in halo_cp:
        cp.start()
    mix(1)
    mix(2)

    row_at = lax.broadcasted_iota(jnp.int32, (256, 240), 0)
    col_at = lax.broadcasted_iota(jnp.int32, (256, 240), 1)
    spread = jnp.where(
        (row_at % 16 < 15) & (col_at == (row_at // 16) * 15 + row_at % 16), 1.0, 0.0
    ).astype(BF)

    def pad_rows(dst, name):
        for b in range(8):
            r, c = (b % 4) * 240, (b // 4) * D
            dst[256 * b : 256 * b + 256, :] = dot(
                spread, s[name][r : r + 240, c : c + D], 1, 0
            ).astype(BF)

    def y_copy(ci, k):
        dz, dy = GROUP[k]
        to = mate(dz, dy)
        return remote(
            s["ysend"].at[ci, :, pl.ds(pl.multiple_of(to * 16, 16), 16)],
            s["yrecv"].at[ci, pl.ds(member * 2, 2)],
            s["y_ss"].at[ci, k], s["y_rs"].at[ci, k], (to, space),
        )

    def g_copy(ci, k):
        dz, dy = GROUP[k]
        to = mate(dz, dy)
        return remote(
            s["gsend"].at[ci, pl.ds(to * 2, 2)],
            s["grecv"].at[ci, :, mine16],
            s["g_ss"].at[ci, k], s["g_rs"].at[ci, k], (to, space),
        )


    def conv_norm(ci):
        i = (ci + 1) % LATD
        r0 = pl.multiple_of(ci * ROWS, ROWS)
        for m in range(MEM):
            for lt in range(D // 128):
                lanes = slice(lt * 128, lt * 128 + 128)
                part = [None] * 3
                for a in range(3):
                    cells = mixed[i + a, m, :, lanes].astype(F32)
                    for b in range(3):
                        term = s["cw"][3 * a + b : 3 * a + b + 1, lanes] * cells
                        part[b] = term if a == 0 else part[b] + term
                s["cbuf"][m * LON : (m + 1) * LON, lanes] = (
                    part[1] + pltpu.roll(part[0], 1, 0) + pltpu.roll(part[2], LON - 1, 0)
                )
        for q in range(ROWS // 32):
            here = slice(q * 32, q * 32 + 32)
            conv = s["cbuf"][here, :]
            center = conv - jnp.mean(conv, axis=-1, keepdims=True)
            inv = lax.rsqrt(jnp.mean(center * center, axis=-1, keepdims=True) + 1e-05)
            normal = center * inv
            s["normal"][ci, here, :] = normal
            s["istd"][ci, here, :] = jnp.broadcast_to(inv, (32, 128))
            s["normed"][pl.ds(pl.multiple_of(r0 + q * 32, 32), 32), :] = (normal * gain).astype(BF)

    def mixer(ci):
        i = (ci + 1) % LATD
        rows = pl.ds(pl.multiple_of(ci * ROWS, ROWS), ROWS)
        normed = s["normed"][rows, :]
        for f in range(4):
            cols = slice(f * 512, f * 512 + 512)
            pre = dot(normed, s["win"][cols, :], 1, 1)
            sq = pre * pre
            t = jnp.tanh(pre * (GC + (GC * 0.044715) * sq))
            half = 0.5 + 0.5 * t
            act = pre * half
            s["activ"][rows, cols] = act.astype(BF)
            s["slope"][rows, cols] = half + act * (1.0 - t) * (GC + (3 * GC * 0.044715) * sq)
        down = dot(s["activ"][rows, :], s["wdn"][...], 1, 0)
        base = mixed[i + 1].reshape(ROWS, D).astype(F32)
        hidden = (base + down).astype(BF)
        s["hidden"][rows, :] = hidden
        pred = dot(hidden, s["whd"][...], 1, 1)
        s["ysend"][ci] = pred.astype(BF).reshape(MEM, LON, OUTC)
        s["yrecv"][ci, pl.ds(member * 2, 2)] = s["ysend"][ci, :, mine16]

    def score(ci):
        i = (ci + 1) % LATD
        for k in range(7):
            y_copy(ci, k).wait_recv()
        yb = s["yrecv"][ci].reshape(256, OUTC)
        gram = dot(yb, yb, 1, 1)
        r = lax.broadcasted_iota(jnp.int32, (256, 256), 0)
        c = lax.broadcasted_iota(jnp.int32, (256, 256), 1)
        diag = jnp.where(r == c, gram, 0.0)
        sq_r = jnp.sum(diag, axis=1, keepdims=True)
        sq_c = jnp.sum(diag, axis=0, keepdims=True)
        inv = lax.rsqrt(jnp.maximum(sq_r + sq_c - 2.0 * gram + 1.0, 1.0))
        w = jnp.where(r % 16 == c % 16, inv, 0.0).astype(BF)
        w_sum = jnp.sum(w.astype(F32), axis=1, keepdims=True)
        pulled = dot(w, yb, 1, 0)
        yf = yb.astype(F32)
        err = (yf.reshape(16, 16, OUTC) - s["tgt"][i, mine16, :][None]).reshape(256, OUTC)
        far = lax.rsqrt(jnp.sum(err * err, axis=-1, keepdims=True) + 1.0)
        grad = err * (far * (SCALE / MEMBERS)) - (yf * w_sum - pulled) * (
            SCALE / (MEMBERS * (MEMBERS - 1))
        )
        s["gsend"][ci] = grad.astype(BF).reshape(MEMBERS, 16, OUTC)
        s["grecv"][ci, :, mine16] = s["gsend"][ci, pl.ds(member * 2, 2)]
        for k in range(7):
            g_copy(ci, k).start()

    for cp in (cw_cp, gain_cp):
        cp.wait()
    s["cacc"][...] = jnp.zeros((10, 8, D), F32)
    gain = s["gain"][...].reshape(1, D)
    conv_norm(0)
    for cp in (*win_cp, *wdn_cp, whd_cp, *tgt_cp):
        cp.wait()
    pad_rows(s["win"], "activ")
    pad_rows(s["wdn"], "gpre")
    for i in range(LATD):
        s["tgt"][i] = traw(i)[...].T

    @pl.loop(0, LATD)
    def _(ci):
        @pl.when(ci == 1)
        def _():
            for cp in halo_cp:
                cp.wait()

            @pl.when(space == 0)
            def _():
                mixed[0] = jnp.zeros((MEM, LON, D), BF)

            @pl.when(space == 15)
            def _():
                mixed[5] = jnp.zeros((MEM, LON, D), BF)

        mixer(ci)
        for k in range(7):
            y_copy(ci, k).start()

        @pl.when(ci < LATD - 1)
        def _():
            conv_norm(ci + 1)

        @pl.when(ci > 1)
        def _():
            score(ci - 2)

    def order(k):
        return CHUNKS[k][3]

    def rs_copy(k, stage, j=1):
        o = order(k)
        if stage == 0:
            n, src, dst, dev = 0, s[f"T{k}"].at[1 - core], s[f"Ra{k}"], partner("c", 1)
        else:
            pair = {1: ("Sb", "Rb"), 2: ("Sc", "Rc"), 3: ("Sd", "Rd")}[stage]
            n = 3 * (stage - 1) + j
            src, dst = s[f"{pair[0]}{k}"].at[j - 1], s[f"{pair[1]}{k}"].at[j - 1]
            dev = partner(o[stage - 1], j)
        return remote(src, dst, s["r_ss"].at[k, n], s["r_rs"].at[k, n], dev)

    def spot(k, o_ylo, o_z, o_yhi, o_x):
        v = {"x": o_x, "y": o_yhi * 2 + o_ylo, "z": o_z}
        return tuple(v[a] for a in order(k))

    def product(k, left, right):
        _, c0, w, _ = CHUNKS[k]
        T = s[f"T{k}"]

        @pl.loop(0, 2)
        def _(o_ylo):
            half = dot(
                left[:, pl.ds(pl.multiple_of(o_ylo * 1024, 1024), 1024)],
                right[0 : LATD * ROWS, c0 : c0 + w],
                0,
                0,
            ).astype(BF)
            for g in range(64):
                o_z, o_yhi, o_x, o_c = g // 16, (g // 8) % 2, (g // 2) % 4, g % 2
                i1, i2, i3 = spot(k, o_ylo, o_z, o_yhi, o_x)
                T[o_c, i1, i2, i3, :, 0:w] = half[g * 16 : g * 16 + 16, :]

    def head_product(k):
        T = s[f"T{k}"]
        grad = dot(s["grecv"][...].reshape(LATD * ROWS, OUTC), s["hidden"][...], 0, 0).astype(BF)
        for t in range(128):
            i1, i2, i3 = spot(k, t // 64, (t // 16) % 4, (t // 8) % 2, (t // 2) % 4)
            rt, ct = t // 5, t % 5
            if t < HEAD_TILES:
                T[t % 2, i1, i2, i3] = grad[rt * 16 : rt * 16 + 16, ct * 128 : ct * 128 + 128]
            else:
                T[t % 2, i1, i2, i3] = jnp.zeros((16, 128), BF)

    def stage1(k):
        a1 = at[order(k)[0]]
        T, Ra, Sb = s[f"T{k}"], s[f"Ra{k}"], s[f"Sb{k}"]
        rs_copy(k, 0).wait_recv()
        for j in (1, 2, 3):
            n = (a1 + j) % 4
            Sb[j - 1] = (T[core, n].astype(F32) + Ra[n].astype(F32)).astype(BF)
            rs_copy(k, 1, j).start()

    def stage2(k):
        a1, a2 = at[order(k)[0]], at[order(k)[1]]
        T, Ra, Rb, Sc = s[f"T{k}"], s[f"Ra{k}"], s[f"Rb{k}"], s[f"Sc{k}"]
        for j in (1, 2, 3):
            rs_copy(k, 1, j).wait_recv()
        for j in (1, 2, 3, 4):
            n = (a2 + j) % 4
            total = T[core, a1, n].astype(F32) + Ra[a1, n].astype(F32)
            for i in range(3):
                total = total + Rb[i, n].astype(F32)
            if j < 4:
                Sc[j - 1] = total.astype(BF)
                rs_copy(k, 2, j).start()
            else:
                s[f"Oc{k}"][...] = total

    def stage3(k):
        a3 = at[order(k)[2]]
        Oc, Rc, Sd = s[f"Oc{k}"], s[f"Rc{k}"], s[f"Sd{k}"]
        for j in (1, 2, 3):
            rs_copy(k, 2, j).wait_recv()
        for j in (1, 2, 3, 4):
            n = (a3 + j) % 4
            total = Oc[n]
            for i in range(3):
                total = total + Rc[i, n].astype(F32)
            Sd[j - 1] = total
            if j < 4:
                rs_copy(k, 3, j).start()

    def finish(k):
        name, c0, w, _ = CHUNKS[k]
        Sd, Rd = s[f"Sd{k}"], s[f"Rd{k}"]
        for j in (1, 2, 3):
            rs_copy(k, 3, j).wait_recv()
        total = Sd[3] + Rd[0] + Rd[1] + Rd[2]
        if name == "head":
            hall[core, h1, h2, h3] = total.astype(BF)
        else:
            out = s["o_gdn"] if name == "down" else s["o_gin"]
            out[:, c0 : c0 + w] = total[0:15, :]

    hall = s["hall"]
    h1, h2, h3 = (at[a] for a in order(0))

    def ag_copy(n, j=1):
        part = [hall.at[core, h1, h2, h3], hall.at[core, h1, h2], hall.at[core, h1], hall.at[core]][n]
        dev = partner("c", 1) if n == 3 else partner(order(0)[2 - n], j)
        m = 9 if n == 3 else 3 * n + j - 1
        return remote(part, part, s["ag_ss"].at[m], s["ag_rs"].at[m], dev)

    def ag_start(n):
        for j in (1,) if n == 3 else (1, 2, 3):
            ag_copy(n, j).start()

    def ag_wait(n):
        for j in (1,) if n == 3 else (1, 2, 3):
            ag_copy(n, j).wait_recv()

    def ar_copy(n, j=1):
        axis = "cxyz"[n]
        buf = s["ar" + axis]
        m = 0 if n == 0 else 3 * n - 3 + j
        part = buf.at[at[axis]]
        return remote(part, part, s["ar_ss"].at[m], s["ar_rs"].at[m], partner(axis, j))

    def ar_start(n, value):
        axis = "cxyz"[n]
        s["ar" + axis][at[axis]] = value
        for j in (1,) if n == 0 else (1, 2, 3):
            ar_copy(n, j).start()

    def ar_sum(n):
        buf = s["ar" + "cxyz"[n]]
        for j in (1,) if n == 0 else (1, 2, 3):
            ar_copy(n, j).wait_recv()
        total = buf[0]
        for i in range(1, 2 if n == 0 else 4):
            total = total + buf[i]
        return total

    def grad_hidden(ci, n):
        rows = pl.ds(pl.multiple_of(ci * ROWS, ROWS), n * ROWS)
        for i in range(n):
            for k in range(7):
                g_copy(ci + i, k).wait_recv()
        s["ghid"][rows, :] = dot(
            s["grecv"][pl.ds(ci, n)].reshape(n * ROWS, OUTC), s["whd"][...], 1, 0
        ).astype(BF)

    def grad_act(ci, n):
        rows = pl.ds(pl.multiple_of(ci * ROWS, ROWS), n * ROWS)
        ghid = s["ghid"][rows, :]
        for f in range(4):
            cols = slice(f * 512, f * 512 + 512)
            gact = dot(ghid, s["wdn"][cols, :], 1, 1)
            s["gpre"][rows, cols] = (s["slope"][rows, cols] * gact).astype(BF)

    def grad_normed(ci, n):
        rows = pl.ds(pl.multiple_of(ci * ROWS, ROWS), n * ROWS)
        s["cbuf"][0 : n * ROWS, :] = dot(s["gpre"][rows, :], s["win"][...], 1, 0)

    def conv_back(ci, r0):
        i = (ci + 1) % LATD
        gain_acc = jnp.zeros((8, D), F32)
        for q in range(ROWS // 32):
            here = slice(q * 32, q * 32 + 32)
            there = slice(r0 + q * 32, r0 + q * 32 + 32)
            gn = s["cbuf"][there, :]
            normal = s["normal"][ci, here, :]
            inv = s["istd"][ci, here, 0:1]
            gain_acc = gain_acc + jnp.sum((gn * normal).reshape(4, 8, D), axis=0)
            g = gn * gain
            s["cbuf"][there, :] = (
                g
                - jnp.mean(g, axis=-1, keepdims=True)
                - normal * jnp.mean(g * normal, axis=-1, keepdims=True)
            ) * inv
        s["cacc"][9] = s["cacc"][9] + gain_acc
        for lt in range(D // 128):
            lanes = slice(lt * 128, lt * 128 + 128)
            acc = [s["cacc"][n, :, lanes] for n in range(9)]
            for m in range(MEM):
                g1 = s["cbuf"][r0 + m * LON : r0 + (m + 1) * LON, lanes]
                moved = [pltpu.roll(g1, LON - 1, 0), g1, pltpu.roll(g1, 1, 0)]
                for a in range(3):
                    cells = mixed[i + a, m, :, lanes].astype(F32)
                    for b in range(3):
                        acc[3 * a + b] = acc[3 * a + b] + jnp.sum(
                            (cells * moved[b]).reshape(16, 8, 128), axis=0
                        )
            for n in range(9):
                s["cacc"][n, :, lanes] = acc[n]

    @pl.loop(0, 3)
    def _(ci):
        @pl.when(ci < 2)
        def _():
            score(ci + 2)

        grad_hidden(ci, 1)
        grad_act(ci, 1)
        grad_normed(ci, 1)
        conv_back(ci, 0)

    def send0(k):
        rs_copy(k, 0).start()

    def sent(*stages):
        for k in range(7):
            for stage in stages:
                for j in (1,) if stage == 0 else (1, 2, 3):
                    rs_copy(k, stage, j).wait_send()

    activ, ghid, gpre, normed = s["activ"], s["ghid"], s["gpre"], s["normed"]
    grad_hidden(3, 1)
    head_product(0)
    send0(0)
    product(1, activ, ghid)
    send0(1)
    stage1(0)
    product(2, activ, ghid)
    send0(2)
    stage1(1)
    product(3, activ, ghid)
    send0(3)
    stage1(2)
    grad_act(3, 1)
    stage1(3)
    product(4, gpre, normed)
    send0(4)
    stage2(0)
    product(5, gpre, normed)
    send0(5)
    stage1(4)
    product(6, gpre, normed)
    send0(6)
    stage1(5)
    stage3(0)
    grad_normed(3, 1)
    stage1(6)
    conv_back(3, 0)
    ar_start(0, jnp.sum(s["cacc"][...], axis=1))
    stage2(1)
    stage2(2)
    stage2(3)
    ar_start(1, ar_sum(0))
    finish(0)
    ag_start(0)

    @pl.loop(0, LATD)
    def _(ci):
        for k in range(7):
            y_copy(ci, k).wait_send()
            g_copy(ci, k).wait_send()

    stage3(1)
    stage3(2)
    ag_wait(0)
    ag_start(1)
    stage3(3)
    stage2(4)
    stage2(5)
    ar_start(2, ar_sum(1))
    stage2(6)
    ag_wait(1)
    ag_start(2)
    finish(1)
    finish(2)
    finish(3)
    out_cp[1].start()
    stage3(4)
    stage3(5)
    ar_start(3, ar_sum(2))
    stage3(6)
    ag_wait(2)
    ag_start(3)
    sent(0, 1)
    sent(2)
    finish(4)
    finish(5)
    finish(6)
    out_cp[0].start()
    ag_wait(3)
    out_cp[2].start()
    sums = ar_sum(3)
    s["o_conv"][...] = sums[0:9]
    s["o_gain"][...] = sums[9, :]
    out_cp[3].start()
    out_cp[4].start()

    sent(3)
    for n in range(4):
        for j in (1,) if n == 3 else (1, 2, 3):
            ag_copy(n, j).wait_send()
        for j in (1,) if n == 0 else (1, 2, 3):
            ar_copy(n, j).wait_send()
    for cp in out_cp:
        cp.wait()


def hand_on(gin, gdn, tiles, gain, conv, gin_out, gdn_out, head_out, gain_out, conv_out):
    gin_out[...] = gin[...]
    gdn_out[...] = gdn[...]
    for t in range(HEAD_TILES):
        v = {"x": (t // 2) % 4, "y": (t // 8) % 2 * 2 + t // 64, "z": (t // 16) % 4}
        i1, i2, i3 = (v[a] for a in CHUNKS[0][3])
        rt, ct = t // 5, t % 5
        head_out[rt * 16 : rt * 16 + 16, ct * 128 : ct * 128 + 128] = tiles[t % 2, i1, i2, i3].astype(F32)
    gain_out[...] = gain[...]
    conv_out[...] = conv[...]


def body(
    latent_state, member_noise, conv_weight, norm_gain, weight_in, weight_down, weight_head, target_field
):
    vmem = pl.BlockSpec(memory_space=pltpu.VMEM)
    hbm = pl.BlockSpec(memory_space=pl.ANY)
    parts = pl.pallas_call(
        kernel,
        name="ensemble_block",
        out_shape=(
            jax.ShapeDtypeStruct((15, D), F32),
            jax.ShapeDtypeStruct((15, D), F32),
            jax.ShapeDtypeStruct((2, 4, 4, 4, 16, 128), BF),
            jax.ShapeDtypeStruct((D,), F32),
            jax.ShapeDtypeStruct((9, D), F32),
        ),
        in_specs=[hbm] * 8,
        out_specs=(hbm,) * 5,
        scratch_shapes=list(scratch().values()),
        compiler_params=pltpu.CompilerParams(
            collective_id=0, has_side_effects=True, vmem_limit_bytes=62 * 2**20
        ),
        cost_estimate=pl.CostEstimate(
            flops=17_000_000_000, bytes_accessed=9_000_000, transcendentals=2_100_000
        ),
    )(
        latent_state, member_noise, conv_weight, norm_gain, weight_in, weight_down,
        weight_head.T, jnp.swapaxes(target_field, 1, 2),
    )
    gin, gdn, head, gain, conv = pl.pallas_call(
        hand_on,
        name="hand_on",
        out_shape=(
            jax.ShapeDtypeStruct((15, D), F32),
            jax.ShapeDtypeStruct((15, D), F32),
            jax.ShapeDtypeStruct((OUTC, D), F32),
            jax.ShapeDtypeStruct((D,), F32),
            jax.ShapeDtypeStruct((9, D), F32),
        ),
        in_specs=[vmem] * 5,
        out_specs=(vmem,) * 5,
        cost_estimate=pl.CostEstimate(flops=0, bytes_accessed=1_900_000, transcendentals=0),
    )(*parts)
    return gin, gdn, head.T, gain, conv


def solution(mesh):
    return jax.shard_map(
        body,
        mesh=mesh,
        in_specs=(
            P("space", None, None),
            P("member", "space", None, None),
            P(),
            P(),
            P(),
            P(),
            P(),
            P("space", None, None),
        ),
        out_specs=(P(("member", "space"), None), P(("member", "space"), None), P(), P(), P()),
        check_vma=False,
    )
```
